128 devices in a mesh: seq: 64 (over y, x, z), batch: 2 (over core).
Axes of the slice: x: 4, y: 4, z: 4, core: 2. Of those that a mesh axis runs over, the one named last changes fastest.
Arguments:
- queries: bfloat16 [2, 32768, 2048], P('batch', 'seq'), may hold values from -24 to 24
- key_vectors: bfloat16 [2, 32768, 2048], P('batch', 'seq'), may hold values from -24 to 24
- values: bfloat16 [2, 32768, 2048], P('batch', 'seq'), may hold values from -8 to 8
- out_grad: bfloat16 [2, 32768, 2048], P('batch', 'seq'), may hold values from -36 to 36
- far_lists: int32 [2, 64, 12], P('batch'), may hold values from 0 to 63, as said below
- level_bias: float32 [3, 16], replicated, may hold values from -1.5 to 1.5
Outputs:
- attended: bfloat16 [2, 32768, 2048], P('batch', 'seq')
- query_grad: bfloat16 [2, 32768, 2048], P('batch', 'seq')
- key_grad: bfloat16 [2, 32768, 2048], P('batch', 'seq')
- value_grad: bfloat16 [2, 32768, 2048], P('batch', 'seq')
- level_grad: float32 [3, 16], replicated
The draws below stay inside these ranges and needn't reach their ends.
Inputs may be any that keep to these rules, and one draw needn't show every extreme that they name: Every row far_lists[b, i] holds 12 different block numbers, none of them i - 1, i or i + 1.
All inputs are finite; a program needn't handle non-finite values.
Results may differ from the reference program's by a relative error of at most 0.024.
Values may be sent and summed in bfloat16 or wider, within the bound.
A program may use at most 192 MiB of HBM per device.

```python
import math
import jax
import jax.numpy as jnp
from jax import lax

HEADS = 16
WIDTH = 2048
LEAF = 512
RIM = 256
TOP_ROWS = 4
SLOTS = 4
LEVELS = 3
BLOCKS = 64
SEQ_LEN = 32768
SEQS = 2


def region_offsets(key):
    region_means = jax.random.truncated_normal(key, -4.0, 4.0, (SEQS, SEQ_LEN // (LEAF // TOP_ROWS), WIDTH), jnp.float32)
    return jnp.repeat(region_means, LEAF // TOP_ROWS, axis=1)


def draw_queries(key, part):
    key = jax.random.fold_in(key, 11)
    sample = jax.random.truncated_normal(key, -4.0, 4.0, (SEQS, SEQ_LEN, WIDTH), jnp.float32)
    return sample.astype(jnp.bfloat16)


def draw_key_vectors(key, part):
    key = jax.random.fold_in(key, 12)
    sample = jax.random.truncated_normal(jax.random.fold_in(key, 1), -4.0, 4.0, (SEQS, SEQ_LEN, WIDTH), jnp.float32)
    sample = sample + region_offsets(jax.random.fold_in(key, 2))
    return sample.astype(jnp.bfloat16)


def draw_values(key, part):
    key = jax.random.fold_in(key, 13)
    sample = jax.random.truncated_normal(jax.random.fold_in(key, 1), -4.0, 4.0, (SEQS, SEQ_LEN, WIDTH), jnp.float32)
    sample = sample + region_offsets(jax.random.fold_in(key, 2))
    return sample.astype(jnp.bfloat16)


def draw_out_grad(key, part):
    key = jax.random.fold_in(key, 14)
    sample = jax.random.truncated_normal(key, -4.0, 4.0, (SEQS, SEQ_LEN, WIDTH), jnp.float32)
    growth = 1.0 + 2.0 * jnp.arange(SEQ_LEN, dtype=jnp.float32) / (SEQ_LEN - 1)
    return (sample * growth[None, :, None]).astype(jnp.bfloat16)


def draw_far_lists(key, part):
    key = jax.random.fold_in(key, 15)
    jitter = jax.random.randint(key, (SEQS, BLOCKS, BLOCKS), 0, 1 << 20)
    reader = jnp.arange(BLOCKS, dtype=jnp.int32)[:, None]
    source = jnp.arange(BLOCKS, dtype=jnp.int32)[None, :]
    nearby = (jnp.abs(reader - source) <= 1).astype(jnp.int32)
    ranking = (jitter + nearby[None] * (1 << 21)) * BLOCKS + source[None]
    picked = jnp.argsort(ranking, axis=-1)[:, :, :3 * SLOTS].astype(jnp.int32)
    distance = jnp.abs(picked - reader[None]) * BLOCKS + picked
    ranked = jnp.argsort(distance, axis=-1)
    return jnp.take_along_axis(picked, ranked, axis=-1).astype(jnp.int32)


def setup_inputs(seed: int = 0) -> dict:
    keys = jax.random.split(jax.random.key(seed), 7)
    return {
        "queries": draw_queries(jax.random.fold_in(keys[6], 71), 0),
        "key_vectors": draw_key_vectors(jax.random.fold_in(keys[6], 71), 0),
        "values": draw_values(jax.random.fold_in(keys[6], 71), 0),
        "out_grad": draw_out_grad(jax.random.fold_in(keys[6], 71), 0),
        "far_lists": draw_far_lists(jax.random.fold_in(keys[6], 71), 0),
        "level_bias": jnp.clip(jax.random.uniform(keys[5], (LEVELS, HEADS), jnp.float32, -1.5, 1.5), -1.5, 1.5),
    }


NEG_FILL = -1e+30

def level_layout(top_rows):
    counts = [top_rows, top_rows // 2, top_rows // 4]
    offsets = [0, top_rows, top_rows + top_rows // 2]
    return (counts, offsets)

def pooled_rows(tokens, top_rows):
    length, feature_width = tokens.shape
    widened = tokens.astype(jnp.float32)
    counts, offsets = level_layout(top_rows)
    pieces = [lax.optimization_barrier(jnp.mean(widened.reshape(row_count, length // row_count, feature_width), axis=1)) for row_count in counts]
    return jnp.concatenate(pieces, axis=0)

def far_bias(level_bias, top_rows, slot_count, leaf_len):
    counts, offsets = level_layout(top_rows)
    columns = []
    for level_no in range(3):
        lifted = level_bias[level_no] + math.log(leaf_len // counts[level_no])
        columns.append(jnp.repeat(lifted[:, None], slot_count * counts[level_no], axis=1))
    return jnp.concatenate(columns, axis=1)

def far_from_table(summary_table, own_list, offsets, counts, slot_count):
    pieces = []
    for level_no in range(3):
        chosen = own_list[level_no * slot_count:(level_no + 1) * slot_count]
        first_row = offsets[level_no]
        picked = summary_table[chosen][:, :, first_row:first_row + counts[level_no]]
        pieces.append(jnp.moveaxis(picked, 0, 1).reshape(2, slot_count * counts[level_no], summary_table.shape[-1]))
    return jnp.concatenate(pieces, axis=1)

def attend_group(packed, score_scale):
    queries, all_keys, all_values, out_grad, key_bias = packed
    query_wide = queries.astype(jnp.float32)
    key_wide = all_keys.astype(jnp.float32)
    value_wide = all_values.astype(jnp.float32)
    grad_wide = out_grad.astype(jnp.float32)
    scores = jnp.einsum('qge,kge->gqk', query_wide, key_wide) * score_scale + key_bias[:, None, :]
    row_max = lax.optimization_barrier(jnp.max(scores, axis=-1, keepdims=True))
    raised = jnp.exp(scores - row_max)
    weights = raised / lax.optimization_barrier(jnp.sum(raised, axis=-1, keepdims=True))
    weights_low = lax.optimization_barrier(weights.astype(jnp.bfloat16))
    weights_wide = weights_low.astype(jnp.float32)
    attended = jnp.einsum('gqk,kge->qge', weights_wide, value_wide).astype(jnp.bfloat16)
    dweights = jnp.einsum('qge,kge->gqk', grad_wide, value_wide)
    row_dot = jnp.einsum('qge,qge->gq', grad_wide, attended.astype(jnp.float32))
    dscores = weights * (dweights - row_dot[:, :, None])
    dscores_low = lax.optimization_barrier(dscores.astype(jnp.bfloat16))
    dscores_wide = dscores_low.astype(jnp.float32)
    query_grad = jnp.einsum('gqk,kge->qge', dscores_wide, key_wide) * score_scale
    key_grad = jnp.einsum('gqk,qge->kge', dscores_wide, query_wide) * score_scale
    value_grad = jnp.einsum('gqk,qge->kge', weights_wide, grad_wide)
    bias_grad = lax.optimization_barrier(jnp.sum(dscores, axis=1))
    return (attended, query_grad, key_grad, value_grad, bias_grad)

def attend_heads(queries, all_keys, all_values, out_grad, key_bias, head_count):
    length, feature_width = queries.shape
    head_dim = feature_width // head_count
    group_size = 4 if head_count % 4 == 0 else head_count
    group_count = head_count // group_size
    score_scale = 1.0 / math.sqrt(head_dim)

    def to_groups(array):
        return jnp.moveaxis(array.reshape(array.shape[0], group_count, group_size, head_dim), 1, 0)

    def from_groups(array):
        return jnp.moveaxis(array, 0, 1).reshape(array.shape[1], feature_width)
    results = lax.map(lambda packed: attend_group(packed, score_scale), (to_groups(queries), to_groups(all_keys), to_groups(all_values), to_groups(out_grad), key_bias.reshape(group_count, group_size, key_bias.shape[1])))
    return (from_groups(results[0]), from_groups(results[1]), from_groups(results[2]), from_groups(results[3]), results[4].reshape(head_count, key_bias.shape[1]))

def one_sequence(queries, key_vectors, values, out_grad, list_rows, level_bias):
    seq_len, feature_width = queries.shape
    blocks = seq_len // LEAF
    head_count = level_bias.shape[1]
    counts, offsets = level_layout(TOP_ROWS)
    near_len = LEAF + 2 * RIM
    pool_keys = jax.vmap(lambda block_rows: pooled_rows(block_rows, TOP_ROWS))(key_vectors.reshape(blocks, LEAF, feature_width))
    pool_values = jax.vmap(lambda block_rows: pooled_rows(block_rows, TOP_ROWS))(values.reshape(blocks, LEAF, feature_width))
    summary_table = jnp.stack([pool_keys, pool_values], axis=1).astype(jnp.bfloat16)
    padded_keys = jnp.pad(key_vectors, ((RIM, RIM), (0, 0)))
    padded_values = jnp.pad(values, ((RIM, RIM), (0, 0)))
    bias_far = far_bias(level_bias, TOP_ROWS, SLOTS, LEAF).astype(jnp.float32)

    def per_block(block_no):
        first_row = block_no * LEAF
        positions = first_row - RIM + jnp.arange(near_len, dtype=jnp.int32)
        inside = (positions >= 0) & (positions < seq_len)
        near_bias = jnp.where(inside, 0.0, NEG_FILL).astype(jnp.float32)
        key_bias = jnp.concatenate([jnp.broadcast_to(near_bias[None, :], (head_count, near_len)), bias_far], axis=1)
        far_pair = far_from_table(summary_table, list_rows[block_no], offsets, counts, SLOTS)
        all_keys = jnp.concatenate([lax.dynamic_slice_in_dim(padded_keys, first_row, near_len, 0), far_pair[0]], axis=0)
        all_values = jnp.concatenate([lax.dynamic_slice_in_dim(padded_values, first_row, near_len, 0), far_pair[1]], axis=0)
        block_queries = lax.dynamic_slice_in_dim(queries, first_row, LEAF, 0)
        block_grad = lax.dynamic_slice_in_dim(out_grad, first_row, LEAF, 0)
        return attend_heads(block_queries, all_keys, all_values, block_grad, key_bias, head_count)
    attended, query_grad, key_terms, value_terms, bias_terms = lax.map(per_block, jnp.arange(blocks, dtype=jnp.int32))

    def settle(terms):
        near_terms = terms[:, :near_len]
        own_terms = near_terms[:, RIM:RIM + LEAF]
        nothing = jnp.zeros_like(near_terms[:1, :RIM])
        from_below = jnp.concatenate([nothing, near_terms[:-1, RIM + LEAF:]], axis=0)
        from_above = jnp.concatenate([near_terms[1:, :RIM], nothing], axis=0)
        own_terms = own_terms.at[:, :RIM].add(from_below).at[:, LEAF - RIM:].add(from_above)
        far_terms = terms[:, near_len:]
        column = 0
        for level_no in range(3):
            row_count = counts[level_no]
            sources = list_rows[:, level_no * SLOTS:(level_no + 1) * SLOTS]
            slot_rows = far_terms[:, column:column + SLOTS * row_count].reshape(blocks, SLOTS, row_count, feature_width)
            summary = jnp.zeros((blocks, row_count, feature_width), far_terms.dtype).at[sources].add(slot_rows)
            pool_length = LEAF // row_count
            own_terms = own_terms + jnp.repeat(summary / pool_length, pool_length, axis=1)
            column += SLOTS * row_count
        return own_terms.reshape(seq_len, feature_width).astype(jnp.bfloat16)
    far_bias_terms = bias_terms[:, :, near_len:]
    level_parts = []
    column = 0
    for level_no in range(3):
        span = SLOTS * counts[level_no]
        level_parts.append(lax.optimization_barrier(jnp.sum(far_bias_terms[:, :, column:column + span], axis=(0, 2))))
        column += span
    return (attended.reshape(seq_len, feature_width), query_grad.reshape(seq_len, feature_width).astype(jnp.bfloat16), settle(key_terms), settle(value_terms), jnp.stack(level_parts))

def reference(queries, key_vectors, values, out_grad, far_lists, level_bias):
    results = [one_sequence(queries[seq_no], key_vectors[seq_no], values[seq_no], out_grad[seq_no], far_lists[seq_no], level_bias) for seq_no in range(queries.shape[0])]
    attended = jnp.stack([entry[0] for entry in results])
    query_grad = jnp.stack([entry[1] for entry in results])
    key_grad = jnp.stack([entry[2] for entry in results])
    value_grad = jnp.stack([entry[3] for entry in results])
    level_total = results[0][4]
    for entry in results[1:]:
        level_total = level_total + entry[4]
    level_grad = level_total / math.sqrt(queries.shape[0] * queries.shape[1])
    return (attended, query_grad, key_grad, value_grad, level_grad)
```

```python
import functools
import math

import jax
import jax.numpy as jnp
from jax import lax
from jax.experimental import pallas as pl
from jax.experimental.pallas import tpu as pltpu
from jax.sharding import PartitionSpec as P

HEADS = 16
DIM = 128
WIDTH = HEADS * DIM
LEAF = 512
RIM = 256
BLOCKS = 64
PAIRS = 8
PAIR = 2 * DIM
NEAR = LEAF + 2 * RIM
FAR = 32
LIST = NEAR + FAR
SCALE = 1.0 / math.sqrt(DIM)
LOG2E = math.log2(math.e)
BIG = 1e30
MESH = pl.DeviceIdType.MESH
F32 = jnp.float32
BF16 = jnp.bfloat16
HALF = WIDTH // 2

NT = (((1,), (1,)), ((), ()))
TN = (((0,), (0,)), ((), ()))
NN = (((1,), (0,)), ((), ()))

CHUNKS = ((0, 256), (256, 256), (512, 256), (768, 256), (1024, FAR))


def dot(a, b, dims=NN):
    return lax.dot_general(a, b, dims, preferred_element_type=F32)


def selector(lists_ref, me):
    row = lax.broadcasted_iota(jnp.int32, (FAR, 4 * BLOCKS), 0)
    col = lax.broadcasted_iota(jnp.int32, (FAR, 4 * BLOCKS), 1)
    block = jnp.full((FAR, 4 * BLOCKS), -1, jnp.int32)
    first = 0
    for level, count in enumerate((4, 2, 1)):
        for slot in range(4):
            listed = lists_ref[me, level * 4 + slot]
            block = jnp.where((row >= first) & (row < first + count), listed, block)
            first += count
    one = (row < 16) & (col == block * 4 + (row & 3))
    two = (row >= 16) & (row < 24) & ((col >> 1) == block * 2 + (row & 1))
    three = (row >= 24) & (row < 28) & ((col >> 2) == block)
    return jnp.where(one, 1.0, 0.0) + jnp.where(two, 0.5, 0.0) + jnp.where(three, 0.25, 0.0)


def kernel(
    q_hbm, k_hbm, v_hbm, g_hbm, lists_ref, bias_ref,
    o_hbm, dq_hbm, dk_hbm, dv_hbm, level_ref,
    kx, vx, qx, gx, ox, dqx, own, to_down, to_up, from_up, from_down,
    table, gtable, zbuf, col32, r1b, r2s, r2b, r3s, r3b, far_grad,
    sel_ref, lvl, lvz, lvx, lvy, lvc, s_ref, w_ref, d_ref,
    fwd_send, fwd_recv, bwd_send, bwd_recv, in_sem, out_sem,
    z_send, z_recv, a1_send, a1_recv, a2_send, a2_recv,
    r1_send, r1_recv, r2_send, r2_recv, r3_send, r3_recv,
    l_send, l_recv, c_send, c_recv,
):
    me = lax.axis_index("seq")
    core = lax.axis_index("batch")
    z = lax.rem(me, 4)
    x = lax.rem(lax.div(me, 4), 4)
    y = lax.div(me, 16)
    up = lax.rem(me + 1, BLOCKS)
    down = lax.rem(me + BLOCKS - 1, BLOCKS)

    def ahead(c, d):
        return lax.rem(c + d, 4)

    def behind(c, d):
        return lax.rem(c + 4 - d, 4)

    def at_y(c):
        return c * 16 + x * 4 + z

    def at_x(c):
        return y * 16 + c * 4 + z

    def at_z(c):
        return y * 16 + x * 4 + c

    def remote(src, dst, send, recv, to):
        return pltpu.make_async_remote_copy(
            src_ref=src, dst_ref=dst, send_sem=send, recv_sem=recv,
            device_id={"seq": to}, device_id_type=MESH,
        )

    barrier = pltpu.get_barrier_semaphore()
    partners = [up, down]
    for d in (1, 2, 3):
        partners += [at_z(ahead(z, d)), at_x(ahead(x, d)), at_y(ahead(y, d))]
    for to in partners:
        pl.semaphore_signal(barrier, inc=1, device_id={"seq": to}, device_id_type=MESH)
    pl.semaphore_signal(barrier, inc=1, device_id={"batch": 1 - core}, device_id_type=MESH)

    def cols(p):
        return pl.ds(pl.multiple_of(p * PAIR, PAIR), PAIR)

    def load(p):
        return [
            pltpu.make_async_copy(k_hbm.at[:, cols(p)], kx.at[p, pl.ds(RIM, LEAF), :], in_sem.at[p, 0]),
            pltpu.make_async_copy(v_hbm.at[:, cols(p)], vx.at[p, pl.ds(RIM, LEAF), :], in_sem.at[p, 1]),
            pltpu.make_async_copy(q_hbm.at[:, cols(p)], qx.at[p], in_sem.at[p, 2]),
            pltpu.make_async_copy(g_hbm.at[:, cols(p)], gx.at[p], in_sem.at[p, 3]),
        ]

    def rims(p):
        lower, upper = pl.ds(0, RIM), pl.ds(RIM, RIM)
        low_rim, high_rim = pl.ds(0, RIM), pl.ds(RIM + LEAF, RIM)
        found = []
        for i, (src, dst) in enumerate(((k_hbm, kx), (v_hbm, vx))):
            found.append(remote(src.at[upper, cols(p)], dst.at[p, low_rim, :], fwd_send.at[p, i, 0], fwd_recv.at[p, i, 0], up))
            found.append(remote(src.at[lower, cols(p)], dst.at[p, high_rim, :], fwd_send.at[p, i, 1], fwd_recv.at[p, i, 1], down))
        return found

    def back(p):
        return [
            remote(to_up.at[p], from_down.at[p], bwd_send.at[p, 0], bwd_recv.at[p, 0], up),
            remote(to_down.at[p], from_up.at[p], bwd_send.at[p, 1], bwd_recv.at[p, 1], down),
        ]

    @pl.loop(0, PAIRS)
    def _(p):
        for c in load(p)[:2]:
            c.start()

    @pl.loop(0, PAIRS)
    def _(p):
        for c in load(p)[2:]:
            c.start()

    pl.semaphore_wait(barrier, 12)
    for c in rims(0):
        c.start()

    sel_ref[...] = selector(lists_ref, me).astype(BF16)

    pool_row = lax.broadcasted_iota(jnp.int32, (8, LEAF), 0)
    pool_tok = lax.broadcasted_iota(jnp.int32, (8, LEAF), 1) // 128
    pool_k = jnp.where(pool_tok == pool_row, 1.0 / 128, 0.0).astype(BF16)
    pool_v = jnp.where(pool_tok + 4 == pool_row, 1.0 / 128, 0.0).astype(BF16)

    @pl.loop(0, PAIRS)
    def _(p):
        for c in load(p)[:2]:
            c.wait()
        mine = pl.ds(RIM, LEAF)
        zbuf[z, :, cols(p)] = dot(pool_k, kx[p, mine, :]) + dot(pool_v, vx[p, mine, :])

    def gather_z(d):
        return remote(zbuf.at[z], zbuf.at[z], z_send.at[d - 1], z_recv.at[d - 1], at_z(ahead(z, d)))

    for d in (1, 2, 3):
        gather_z(d).start()
    @pl.loop(1, PAIRS)
    def _(p):
        for c in rims(p):
            c.start()

    for d in (1, 2, 3):
        gather_z(d).wait_recv()
    for i in (0, 1):
        for c in range(4):
            col32[4 * c : 4 * c + 4, :] = zbuf[c, 4 * i : 4 * i + 4, :]
        table[i, y, x] = col32[...].astype(BF16)

    def gather_one(d):
        return [
            remote(table.at[0, y, x], table.at[0, y, x], a1_send.at[0, d - 1], a1_recv.at[0, d - 1], at_x(ahead(x, d))),
            remote(table.at[1, y, x], table.at[1, y, x], a1_send.at[1, d - 1], a1_recv.at[1, d - 1], at_y(ahead(y, d))),
        ]

    def gather_two(d):
        return [
            remote(table.at[0, y], table.at[0, y], a2_send.at[0, d - 1], a2_recv.at[0, d - 1], at_y(ahead(y, d))),
            remote(table.at[1, :, x], table.at[1, :, x], a2_send.at[1, d - 1], a2_recv.at[1, d - 1], at_x(ahead(x, d))),
        ]

    for d in (1, 2, 3):
        for c in gather_one(d):
            c.start()
    for d in (1, 2, 3):
        for c in gather_one(d):
            c.wait_recv()
    for d in (1, 2, 3):
        for c in gather_two(d):
            c.start()
    for d in (1, 2, 3):
        for c in gather_two(d):
            c.wait_recv()

    lane_sel = lax.broadcasted_iota(jnp.int32, (FAR, 128), 1)
    far_row = lax.broadcasted_iota(jnp.int32, (FAR, 1), 0)
    lvl[...] = jnp.zeros_like(lvl)
    low_gap = jnp.where(me == 0, BIG, 0.0).astype(F32)
    high_gap = jnp.where(me == BLOCKS - 1, BIG, 0.0).astype(F32)
    gaps = (low_gap, None, None, high_gap, None)
    factor = SCALE * LOG2E

    def head(p, h):
        lanes = slice(h * DIM, h * DIM + DIM)
        head_no = 2 * p + h
        bias = jnp.where(
            far_row < 16, bias_ref[0, head_no] + math.log(128),
            jnp.where(far_row < 24, bias_ref[1, head_no] + math.log(256),
                      jnp.where(far_row < 28, bias_ref[2, head_no] + math.log(512), -BIG)))
        bias = bias * LOG2E
        query = qx[p, :, lanes]
        grad = gx[p, :, lanes]
        top = None
        for (first, rows), gap in zip(CHUNKS, gaps):
            s = dot(kx[p, first : first + rows, lanes], query, NT) * factor
            if rows == FAR:
                s = s + bias
            s_ref[h, first : first + rows, :] = s
            peak = jnp.max(s, axis=0, keepdims=True)
            if gap is not None:
                peak = peak - gap
            top = peak if top is None else jnp.maximum(top, peak)
        total = jnp.zeros((1, LEAF), F32)
        for (first, rows), gap in zip(CHUNKS, gaps):
            base = top if gap is None else top + gap
            e = jnp.exp2(s_ref[h, first : first + rows, :] - base)
            s_ref[h, first : first + rows, :] = e
            total = total + jnp.sum(e, axis=0, keepdims=True)
        inverse = 1.0 / total
        for first, rows in CHUNKS:
            w_ref[h, first : first + rows, :] = (s_ref[h, first : first + rows, :] * inverse).astype(BF16)
        out = dot(vx[p, :, lanes], w_ref[h], TN).T.astype(BF16)
        ox[p, :, lanes] = out
        ones = jnp.ones((8, DIM), F32)
        row_dot = lax.dot_general(
            ones, out.astype(F32) * grad.astype(F32), NT,
            precision=lax.Precision.HIGHEST, preferred_element_type=F32)[0:1, :]
        for first, rows in CHUNKS:
            dw = dot(vx[p, first : first + rows, lanes], grad, NT)
            ds = s_ref[h, first : first + rows, :] * inverse * (dw - row_dot)
            d_ref[h, first : first + rows, :] = ds.astype(BF16)
            if rows == FAR:
                sums = jnp.sum(ds, axis=1, keepdims=True)
                lvl[...] += jnp.where(lane_sel == head_no, sums, 0.0)
        dqx[p, :, lanes] = (dot(kx[p, :, lanes], d_ref[h], TN) * SCALE).T.astype(BF16)
        dk = dot(d_ref[h], query) * SCALE
        dv = dot(w_ref[h], grad)
        for i, term in enumerate((dk, dv)):
            to_down[p, i, :, lanes] = term[:RIM].astype(BF16)
            own[p, i, :, lanes] = term[RIM : RIM + LEAF]
            to_up[p, i, :, lanes] = term[RIM + LEAF : NEAR].astype(BF16)
        return dk[NEAR:], dv[NEAR:]

    def half_lanes(half):
        return pl.ds(half * HALF, HALF)

    def r1(half, d):
        n = half_lanes(half)
        yp, xp = ahead(y, d), ahead(x, d)
        return [
            remote(gtable.at[0, yp, :, :, n], r1b.at[0, y, :, :, n], r1_send.at[half, 0, d - 1], r1_recv.at[half, 0, d - 1], at_y(yp)),
            remote(gtable.at[1, :, xp, :, n], r1b.at[1, x, :, :, n], r1_send.at[half, 1, d - 1], r1_recv.at[half, 1, d - 1], at_x(xp)),
        ]

    def r2(half, d):
        n = half_lanes(half)
        yp, xp = ahead(y, d), ahead(x, d)
        return [
            remote(r2s.at[0, xp, :, n], r2b.at[0, x, :, n], r2_send.at[half, 0, d - 1], r2_recv.at[half, 0, d - 1], at_x(xp)),
            remote(r2s.at[1, yp, :, n], r2b.at[1, y, :, n], r2_send.at[half, 1, d - 1], r2_recv.at[half, 1, d - 1], at_y(yp)),
        ]

    def r3(half, d):
        n = half_lanes(half)
        zp = ahead(z, d)
        return [remote(r3s.at[zp, :, n], r3b.at[z, :, n], r3_send.at[half, d - 1], r3_recv.at[half, d - 1], at_z(zp))]

    def go(step, half):
        for d in (1, 2, 3):
            for c in step(half, d):
                c.start()

    def got(step, half):
        for d in (1, 2, 3):
            for c in step(half, d):
                c.wait_recv()

    def r1_finish(half):
        n = half_lanes(half)
        got(r1, half)
        for i in range(4):
            sum_k = gtable[0, y, i, :, n].astype(F32)
            sum_v = gtable[1, i, x, :, n].astype(F32)
            for d in (1, 2, 3):
                sum_k = sum_k + r1b[0, behind(y, d), i, :, n].astype(F32)
                sum_v = sum_v + r1b[1, behind(x, d), i, :, n].astype(F32)
            r2s[0, i, :, n] = sum_k.astype(BF16)
            r2s[1, i, :, n] = sum_v.astype(BF16)
        go(r2, half)

    def r2_finish(half):
        n = half_lanes(half)
        got(r2, half)
        for j, c in enumerate((x, y)):
            total = r2s[j, c, :, n].astype(F32)
            for d in (1, 2, 3):
                total = total + r2b[j, behind(c, d), :, n].astype(F32)
            col32[:, n] = total
            for i in range(4):
                r3s[i, 4 * j : 4 * j + 4, n] = col32[4 * i : 4 * i + 4, n]
        go(r3, half)

    def r3_finish(half):
        n = half_lanes(half)
        got(r3, half)
        total = r3s[z, :, n]
        for d in (1, 2, 3):
            total = total + r3b[behind(z, d), :, n]
        far_grad[:, n] = total * (1.0 / 128)

    def outs(p):
        return [
            pltpu.make_async_copy(ox.at[p], o_hbm.at[:, cols(p)], out_sem.at[p, 0]),
            pltpu.make_async_copy(dqx.at[p], dq_hbm.at[:, cols(p)], out_sem.at[p, 1]),
            pltpu.make_async_copy(qx.at[p], dk_hbm.at[:, cols(p)], out_sem.at[p, 2]),
            pltpu.make_async_copy(gx.at[p], dv_hbm.at[:, cols(p)], out_sem.at[p, 3]),
        ]

    @pl.loop(0, PAIRS)
    def _(p):
        sel = sel_ref[...]
        for i, dst in enumerate((kx, vx)):
            rows = table[i, :, :, :, cols(p)].reshape(4 * BLOCKS, PAIR)
            dst[p, NEAR:LIST, :] = dot(sel, rows).astype(BF16)
        for c in load(p)[2:]:
            c.wait()
        for c in rims(p):
            c.wait_recv()
        first = head(p, 0)
        second = head(p, 1)
        for c in back(p):
            c.start()
        for c in outs(p)[:2]:
            c.start()
        for i in (0, 1):
            rows = jnp.concatenate([first[i], second[i]], axis=1).astype(BF16)
            gtable[i, :, :, :, cols(p)] = dot(sel, rows, TN).astype(BF16).reshape(4, 4, 16, PAIR)

        @pl.when(p == 3)
        def _():
            go(r1, 0)

        @pl.when(p == 4)
        def _():
            r1_finish(0)

        @pl.when(p == 5)
        def _():
            r2_finish(0)

    go(r1, 1)

    level_no = lax.broadcasted_iota(jnp.int32, (8, FAR), 0)
    list_row = lax.broadcasted_iota(jnp.int32, (8, FAR), 1)
    level_of = jnp.where(list_row < 16, 0, jnp.where(list_row < 24, 1, jnp.where(list_row < 28, 2, 9)))
    pick = jnp.where(level_no == level_of, 1.0, 0.0).astype(F32)
    lvy[y] = lax.dot_general(pick, lvl[...], NN, precision=lax.Precision.HIGHEST, preferred_element_type=F32)

    def level_copy(buf, c, step, d, to):
        return remote(buf.at[c], buf.at[c], l_send.at[step, d - 1], l_recv.at[step, d - 1], to)

    def level_steps(step):
        buf, c, at = ((lvy, y, at_y), (lvx, x, at_x), (lvz, z, at_z))[step]
        return [level_copy(buf, c, step, d, at(ahead(c, d))) for d in (1, 2, 3)]

    def level_sum(step):
        for c in level_steps(step):
            c.wait_recv()
        buf = (lvy, lvx, lvz)[step]
        return (buf[0] + buf[1]) + (buf[2] + buf[3])

    for c in level_steps(0):
        c.start()

    def settle(p):
        for c in back(p):
            c.wait_recv()
        for i, dst in enumerate((qx, gx)):
            for r in range(4):
                tokens = pl.ds(128 * r, 128)
                total = own[p, i, tokens, :] + far_grad[4 * i + r : 4 * i + r + 1, cols(p)]
                if r < 2:
                    total = total + from_down[p, i, tokens, :].astype(F32)
                else:
                    total = total + from_up[p, i, pl.ds(128 * (r - 2), 128), :].astype(F32)
                dst[p, tokens, :] = total.astype(BF16)
        for c in outs(p)[2:]:
            c.start()

    r3_finish(0)

    @pl.loop(0, 4)
    def _(p):
        settle(p)

    lvx[x] = level_sum(0)
    for c in level_steps(1):
        c.start()
    r1_finish(1)
    lvz[z] = level_sum(1)
    for c in level_steps(2):
        c.start()
    r2_finish(1)
    lvc[core] = level_sum(2)
    swap = pltpu.make_async_remote_copy(
        src_ref=lvc.at[core], dst_ref=lvc.at[core], send_sem=c_send, recv_sem=c_recv,
        device_id={"batch": 1 - core}, device_id_type=MESH)
    swap.start()
    r3_finish(1)

    @pl.loop(4, PAIRS)
    def _(p):
        settle(p)

    swap.wait_recv()
    level_ref[...] = ((lvc[0] + lvc[1]) * (1.0 / math.sqrt(2 * BLOCKS * LEAF)))[0:3, 0:HEADS]

    swap.wait_send()
    for step in range(3):
        for c in level_steps(step):
            c.wait_send()
    for d in (1, 2, 3):
        gather_z(d).wait_send()
        for c in gather_one(d) + gather_two(d):
            c.wait_send()
        for half in (0, 1):
            for c in r1(half, d) + r2(half, d) + r3(half, d):
                c.wait_send()

    @pl.loop(0, PAIRS)
    def _(p):
        for c in rims(p) + back(p):
            c.wait_send()
        for c in outs(p):
            c.wait()


def shards(queries, key_vectors, values, out_grad, far_lists, level_bias):
    any_spec = pl.BlockSpec(memory_space=pl.ANY)
    smem = pl.BlockSpec(memory_space=pltpu.SMEM)
    dma = pltpu.SemaphoreType.DMA
    outs = pl.pallas_call(
        kernel,
        out_shape=[jax.ShapeDtypeStruct((LEAF, WIDTH), BF16)] * 4 + [jax.ShapeDtypeStruct((3, HEADS), F32)],
        in_specs=[any_spec] * 4 + [smem] * 2,
        out_specs=[any_spec] * 4 + [pl.BlockSpec(memory_space=pltpu.VMEM)],
        scratch_shapes=[
            pltpu.VMEM((PAIRS, LIST, PAIR), BF16),
            pltpu.VMEM((PAIRS, LIST, PAIR), BF16),
            pltpu.VMEM((PAIRS, LEAF, PAIR), BF16),
            pltpu.VMEM((PAIRS, LEAF, PAIR), BF16),
            pltpu.VMEM((PAIRS, LEAF, PAIR), BF16),
            pltpu.VMEM((PAIRS, LEAF, PAIR), BF16),
            pltpu.VMEM((PAIRS, 2, LEAF, PAIR), F32),
            pltpu.VMEM((PAIRS, 2, RIM, PAIR), BF16),
            pltpu.VMEM((PAIRS, 2, RIM, PAIR), BF16),
            pltpu.VMEM((PAIRS, 2, RIM, PAIR), BF16),
            pltpu.VMEM((PAIRS, 2, RIM, PAIR), BF16),
            pltpu.VMEM((2, 4, 4, 16, WIDTH), BF16),
            pltpu.VMEM((2, 4, 4, 16, WIDTH), BF16),
            pltpu.VMEM((4, 8, WIDTH), F32),
            pltpu.VMEM((16, WIDTH), F32),
            pltpu.VMEM((2, 4, 4, 16, WIDTH), BF16),
            pltpu.VMEM((2, 4, 16, WIDTH), BF16),
            pltpu.VMEM((2, 4, 16, WIDTH), BF16),
            pltpu.VMEM((4, 8, WIDTH), F32),
            pltpu.VMEM((4, 8, WIDTH), F32),
            pltpu.VMEM((8, WIDTH), F32),
            pltpu.VMEM((FAR, 4 * BLOCKS), BF16),
            pltpu.VMEM((FAR, 128), F32),
            pltpu.VMEM((4, 8, 128), F32),
            pltpu.VMEM((4, 8, 128), F32),
            pltpu.VMEM((4, 8, 128), F32),
            pltpu.VMEM((2, 8, 128), F32),
            pltpu.VMEM((2, LIST, LEAF), F32),
            pltpu.VMEM((2, LIST, LEAF), BF16),
            pltpu.VMEM((2, LIST, LEAF), BF16),
            dma((PAIRS, 2, 2)), dma((PAIRS, 2, 2)), dma((PAIRS, 2)), dma((PAIRS, 2)),
            dma((PAIRS, 4)), dma((PAIRS, 4)),
            dma((3,)), dma((3,)), dma((2, 3)), dma((2, 3)), dma((2, 3)), dma((2, 3)),
            dma((2, 2, 3)), dma((2, 2, 3)), dma((2, 2, 3)), dma((2, 2, 3)), dma((2, 3)), dma((2, 3)),
            dma((3, 3)), dma((3, 3)), dma, dma,
        ],
        compiler_params=pltpu.CompilerParams(
            collective_id=0, has_side_effects=True, vmem_limit_bytes=62 * 1024 * 1024),
        cost_estimate=pl.CostEstimate(
            flops=12 * HEADS * LEAF * LIST * DIM, bytes_accessed=8 * LEAF * WIDTH * 2,
            transcendentals=HEADS * LEAF * LIST),
    )(queries[0], key_vectors[0], values[0], out_grad[0], far_lists[0], level_bias)
    return tuple(o[None] for o in outs[:4]) + (outs[4],)


def solution(mesh):
    token = P("batch", "seq", None)
    return jax.shard_map(
        shards,
        mesh=mesh,
        in_specs=(token, token, token, token, P("batch", None, None), P()),
        out_specs=(token, token, token, token, P()),
        check_vma=False,
    )
```

```python
import functools
import math

import jax
import jax.numpy as jnp
from jax import lax
from jax.experimental import pallas as pl
from jax.experimental.pallas import tpu as pltpu
from jax.sharding import PartitionSpec as P

HEADS = 16
DIM = 128
WIDTH = HEADS * DIM
LEAF = 512
RIM = 256
BLOCKS = 64
PAIRS = 8
PAIR = 2 * DIM
NEAR = LEAF + 2 * RIM
FAR = 32
LIST = NEAR + FAR
SCALE = 1.0 / math.sqrt(DIM)
LOG2E = math.log2(math.e)
BIG = 1e30
MESH = pl.DeviceIdType.MESH
F32 = jnp.float32
BF16 = jnp.bfloat16
HALF = WIDTH // 2

NT = (((1,), (1,)), ((), ()))
TN = (((0,), (0,)), ((), ()))
NN = (((1,), (0,)), ((), ()))

CHUNKS = ((0, 256), (256, 256), (512, 256), (768, 256), (1024, FAR))


def dot(a, b, dims=NN):
    return lax.dot_general(a, b, dims, preferred_element_type=F32)


def selector(lists_ref, reader, block):
    shape = (FAR, 64)
    row = lax.broadcasted_iota(jnp.int32, shape, 0)
    col = lax.broadcasted_iota(jnp.int32, shape, 1)
    wanted = jnp.full(shape, -1, jnp.int32)
    first = 0
    for level, count in enumerate((4, 2, 1)):
        for slot in range(4):
            listed = lists_ref[reader, level * 4 + slot]
            wanted = jnp.where((row >= first) & (row < first + count), listed, wanted)
            first += count
    part = col & 3
    one = (row < 16) & (part == (row & 3))
    two = (row >= 16) & (row < 24) & ((part >> 1) == (row & 1))
    share = jnp.where(one, 1.0, 0.0) + jnp.where(two, 0.5, 0.0) + jnp.where(row >= 24, 0.25, 0.0)
    return jnp.where(wanted == block, share, 0.0).astype(BF16)


def kernel(
    q_hbm, k_hbm, v_hbm, g_hbm, lists_ref, bias_ref,
    o_hbm, dq_hbm, dk_hbm, dv_hbm, level_ref,
    kx, vx, qx, gx, ox, dqx, own, to_down, to_up, from_up, from_down,
    table, chosen, listed, dlisted, zbuf, col32, r2s, r2b, r3s, r3b, far_grad,
    sel_ref, lvl, lvz, lvx, lvy, lvc, s_ref, w_ref, d_ref,
    fwd_relay, bwd_relay, relay_send, relay_recv,
    fwd_send, fwd_recv, bwd_send, bwd_recv, in_sem, out_sem,
    z_send, z_recv, a1_send, a1_recv, a2_send, a2_recv,
    r1_send, r1_recv, r2_send, r2_recv, r3_send, r3_recv,
    l_send, l_recv, c_send, c_recv,
):
    me = lax.axis_index("seq")
    core = lax.axis_index("batch")
    z = lax.rem(me, 4)
    x = lax.rem(lax.div(me, 4), 4)
    y = lax.div(me, 16)
    up = lax.rem(me + 1, BLOCKS)
    down = lax.rem(me + BLOCKS - 1, BLOCKS)
    next_z = lax.rem(me + 4, BLOCKS)
    last_z = lax.rem(me + BLOCKS - 4, BLOCKS)

    def ahead(c, d):
        return lax.rem(c + d, 4)

    def behind(c, d):
        return lax.rem(c + 4 - d, 4)

    def at_y(c):
        return c * 16 + x * 4 + z

    def at_x(c):
        return y * 16 + c * 4 + z

    def at_z(c):
        return y * 16 + x * 4 + c

    def remote(src, dst, send, recv, to):
        return pltpu.make_async_remote_copy(
            src_ref=src, dst_ref=dst, send_sem=send, recv_sem=recv,
            device_id={"seq": to}, device_id_type=MESH,
        )

    barrier = pltpu.get_barrier_semaphore()
    partners = [up, down, next_z, last_z]
    for d in (1, 2, 3):
        partners += [at_z(ahead(z, d)), at_x(ahead(x, d)), at_y(ahead(y, d))]
    for to in partners:
        pl.semaphore_signal(barrier, inc=1, device_id={"seq": to}, device_id_type=MESH)
    pl.semaphore_signal(barrier, inc=1, device_id={"batch": 1 - core}, device_id_type=MESH)

    def cols(p):
        return pl.ds(pl.multiple_of(p * PAIR, PAIR), PAIR)

    def load(p):
        return [
            pltpu.make_async_copy(k_hbm.at[:, cols(p)], kx.at[p, pl.ds(RIM, LEAF), :], in_sem.at[p, 0]),
            pltpu.make_async_copy(v_hbm.at[:, cols(p)], vx.at[p, pl.ds(RIM, LEAF), :], in_sem.at[p, 1]),
            pltpu.make_async_copy(q_hbm.at[:, cols(p)], qx.at[p], in_sem.at[p, 2]),
            pltpu.make_async_copy(g_hbm.at[:, cols(p)], gx.at[p], in_sem.at[p, 3]),
        ]

    low_rim, high_rim = pl.ds(0, RIM), pl.ds(RIM + LEAF, RIM)

    def rims(p):
        lower, upper = pl.ds(0, RIM), pl.ds(RIM, RIM)
        found = []
        for i, (src, dst) in enumerate(((k_hbm, kx), (v_hbm, vx))):
            found.append(remote(src.at[upper, cols(p)], dst.at[p, low_rim, :], fwd_send.at[p, i, 0], fwd_recv.at[p, i, 0], up))
            found.append(remote(src.at[lower, cols(p)], dst.at[p, high_rim, :], fwd_send.at[p, i, 1], fwd_recv.at[p, i, 1], down))
        return found

    def back(p):
        found = []
        for i in (0, 1):
            found.append(remote(to_up.at[p, i], from_down.at[p, i], bwd_send.at[p, i, 0], bwd_recv.at[p, i, 0], up))
            found.append(remote(to_down.at[p, i], from_up.at[p, i], bwd_send.at[p, i, 1], bwd_recv.at[p, i, 1], down))
        return found

    def detour(p, backward):
        if backward:
            sources, held, send, recv = (to_up.at[p, 1], to_down.at[p, 1]), bwd_relay.at[p], bwd_send, relay_recv.at[p, 1]
        else:
            sources = (v_hbm.at[pl.ds(RIM, RIM), cols(p)], v_hbm.at[pl.ds(0, RIM), cols(p)])
            held, send, recv = fwd_relay.at[p], fwd_send, relay_recv.at[p, 0]
        return (remote(sources[0], held, send.at[p, 1, 0], recv, at_z(0)),
                remote(sources[1], held, send.at[p, 1, 1], recv, at_z(3)))

    def onward(p, backward):
        if backward:
            held, send = bwd_relay.at[p], relay_send.at[p, 1]
            return (remote(held, from_down.at[p, 1], send, bwd_recv.at[p, 1, 0], next_z),
                    remote(held, from_up.at[p, 1], send, bwd_recv.at[p, 1, 1], last_z))
        held, send = fwd_relay.at[p], relay_send.at[p, 0]
        return (remote(held, vx.at[p, low_rim, :], send, fwd_recv.at[p, 1, 0], next_z),
                remote(held, vx.at[p, high_rim, :], send, fwd_recv.at[p, 1, 1], last_z))

    def send_out(p, backward):
        key_up, key_down, value_up, value_down = back(p) if backward else rims(p)
        far_up, far_down = detour(p, backward)
        key_up.start()
        key_down.start()

        @pl.when(z == 3)
        def _():
            far_up.start()

        @pl.when(z != 3)
        def _():
            value_up.start()

        @pl.when(z == 0)
        def _():
            far_down.start()

        @pl.when(z != 0)
        def _():
            value_down.start()

    def relay(p, backward):
        came_up, came_down = detour(p, backward)
        on_up, on_down = onward(p, backward)

        @pl.when(z == 0)
        def _():
            came_up.wait_recv()
            on_up.start()

        @pl.when(z == 3)
        def _():
            came_down.wait_recv()
            on_down.start()

    @pl.loop(0, PAIRS)
    def _(p):
        for c in load(p)[:2]:
            c.start()

    @pl.loop(0, PAIRS)
    def _(p):
        for c in load(p)[2:]:
            c.start()

    pl.semaphore_wait(barrier, 14)
    send_out(0, False)

    col_block = lax.broadcasted_iota(jnp.int32, (FAR, 64), 1) // 4
    key_block = y * 16 + col_block
    value_block = (col_block // 4) * 16 + x * 4 + (col_block & 3)
    for i in range(4):
        sel_ref[0, i * FAR : (i + 1) * FAR, :] = selector(lists_ref, at_y(i), key_block)
        sel_ref[1, i * FAR : (i + 1) * FAR, :] = selector(lists_ref, at_x(i), value_block)

    pool_row = lax.broadcasted_iota(jnp.int32, (8, LEAF), 0)
    pool_tok = lax.broadcasted_iota(jnp.int32, (8, LEAF), 1) // 128
    pool_k = jnp.where(pool_tok == pool_row, 1.0 / 128, 0.0).astype(BF16)
    pool_v = jnp.where(pool_tok + 4 == pool_row, 1.0 / 128, 0.0).astype(BF16)

    @pl.loop(0, PAIRS)
    def _(p):
        for c in load(p)[:2]:
            c.wait()
        mine = pl.ds(RIM, LEAF)
        zbuf[z, :, cols(p)] = dot(pool_k, kx[p, mine, :]) + dot(pool_v, vx[p, mine, :])

    def gather_z(d):
        return remote(zbuf.at[z], zbuf.at[z], z_send.at[d - 1], z_recv.at[d - 1], at_z(ahead(z, d)))

    for d in (1, 2, 3):
        gather_z(d).start()
    for d in (1, 2, 3):
        gather_z(d).wait_recv()
    for i in (0, 1):
        for c in range(4):
            col32[4 * c : 4 * c + 4, :] = zbuf[c, 4 * i : 4 * i + 4, :]
        table[i, (x, y)[i]] = col32[...].astype(BF16)

    def gather_one(d):
        return [
            remote(table.at[0, x], table.at[0, x], a1_send.at[0, d - 1], a1_recv.at[0, d - 1], at_x(ahead(x, d))),
            remote(table.at[1, y], table.at[1, y], a1_send.at[1, d - 1], a1_recv.at[1, d - 1], at_y(ahead(y, d))),
        ]

    def gather_two(d):
        yp, xp = ahead(y, d), ahead(x, d)
        return [
            remote(chosen.at[0, yp], listed.at[0, y], a2_send.at[0, d - 1], a2_recv.at[0, d - 1], at_y(yp)),
            remote(chosen.at[1, xp], listed.at[1, x], a2_send.at[1, d - 1], a2_recv.at[1, d - 1], at_x(xp)),
        ]

    for d in (1, 2, 3):
        for c in gather_one(d):
            c.start()
    send_out(1, False)
    for d in (1, 2, 3):
        for c in gather_one(d):
            c.wait_recv()
    for i in (0, 1):
        for n in range(0, WIDTH, 512):
            rows = table[i, :, :, n : n + 512].reshape(64, 512)
            chosen[i, :, :, n : n + 512] = dot(sel_ref[i], rows).astype(BF16).reshape(4, FAR, 512)
    for d in (1, 2, 3):
        for c in gather_two(d):
            c.start()
    listed[0, y] = chosen[0, y]
    listed[1, x] = chosen[1, x]

    @pl.loop(2, PAIRS)
    def _(p):
        send_out(p, False)

    for d in (1, 2, 3):
        for c in gather_two(d):
            c.wait_recv()

    for p in range(3):
        relay(p, False)

    lane_sel = lax.broadcasted_iota(jnp.int32, (FAR, 128), 1)
    far_row = lax.broadcasted_iota(jnp.int32, (FAR, 1), 0)
    lvl[...] = jnp.zeros_like(lvl)
    low_gap = jnp.where(me == 0, BIG, 0.0).astype(F32)
    high_gap = jnp.where(me == BLOCKS - 1, BIG, 0.0).astype(F32)
    gaps = (low_gap, None, None, high_gap, None)
    factor = SCALE * LOG2E

    def head(p, h):
        lanes = slice(h * DIM, h * DIM + DIM)
        head_no = 2 * p + h
        bias = jnp.where(
            far_row < 16, bias_ref[0, head_no] + math.log(128),
            jnp.where(far_row < 24, bias_ref[1, head_no] + math.log(256),
                      jnp.where(far_row < 28, bias_ref[2, head_no] + math.log(512), -BIG)))
        bias = bias * LOG2E
        query = qx[p, :, lanes]
        grad = gx[p, :, lanes]
        top = None
        for (first, rows), gap in zip(CHUNKS, gaps):
            s = dot(kx[p, first : first + rows, lanes], query, NT) * factor
            if rows == FAR:
                s = s + bias
            s_ref[h, first : first + rows, :] = s
            peak = jnp.max(s, axis=0, keepdims=True)
            if gap is not None:
                peak = peak - gap
            top = peak if top is None else jnp.maximum(top, peak)
        total = jnp.zeros((1, LEAF), F32)
        for (first, rows), gap in zip(CHUNKS, gaps):
            base = top if gap is None else top + gap
            e = jnp.exp2(s_ref[h, first : first + rows, :] - base)
            s_ref[h, first : first + rows, :] = e
            total = total + jnp.sum(e, axis=0, keepdims=True)
        inverse = 1.0 / total
        for first, rows in CHUNKS:
            w_ref[h, first : first + rows, :] = (s_ref[h, first : first + rows, :] * inverse).astype(BF16)
        out = dot(vx[p, :, lanes], w_ref[h], TN).T.astype(BF16)
        ox[p, :, lanes] = out
        ones = jnp.ones((8, DIM), F32)
        row_dot = lax.dot_general(
            ones, out.astype(F32) * grad.astype(F32), NT,
            precision=lax.Precision.HIGHEST, preferred_element_type=F32)[0:1, :]
        for first, rows in CHUNKS:
            dw = dot(vx[p, first : first + rows, lanes], grad, NT)
            ds = s_ref[h, first : first + rows, :] * inverse * (dw - row_dot)
            d_ref[h, first : first + rows, :] = ds.astype(BF16)
            if rows == FAR:
                sums = jnp.sum(ds, axis=1, keepdims=True)
                lvl[...] += jnp.where(lane_sel == head_no, sums, 0.0)
        dqx[p, :, lanes] = (dot(kx[p, :, lanes], d_ref[h], TN) * SCALE).T.astype(BF16)
        dk = dot(d_ref[h], query) * SCALE
        dv = dot(w_ref[h], grad)
        for i, term in enumerate((dk, dv)):
            to_down[p, i, :, lanes] = term[:RIM].astype(BF16)
            own[p, i, :, lanes] = term[RIM : RIM + LEAF]
            to_up[p, i, :, lanes] = term[RIM + LEAF : NEAR].astype(BF16)
        return dk[NEAR:], dv[NEAR:]

    def half_lanes(half):
        return pl.ds(half * HALF, HALF)

    def r1(half, d):
        n = half_lanes(half)
        yp, xp = ahead(y, d), ahead(x, d)
        return [
            remote(dlisted.at[0, y, :, n], dlisted.at[0, y, :, n], r1_send.at[half, 0, d - 1], r1_recv.at[half, 0, d - 1], at_y(yp)),
            remote(dlisted.at[1, x, :, n], dlisted.at[1, x, :, n], r1_send.at[half, 1, d - 1], r1_recv.at[half, 1, d - 1], at_x(xp)),
        ]

    def r2(half, d):
        n = half_lanes(half)
        yp, xp = ahead(y, d), ahead(x, d)
        return [
            remote(r2s.at[0, xp, :, n], r2b.at[0, x, :, n], r2_send.at[half, 0, d - 1], r2_recv.at[half, 0, d - 1], at_x(xp)),
            remote(r2s.at[1, yp, :, n], r2b.at[1, y, :, n], r2_send.at[half, 1, d - 1], r2_recv.at[half, 1, d - 1], at_y(yp)),
        ]

    def r3(half, d):
        n = half_lanes(half)
        zp = ahead(z, d)
        return [remote(r3s.at[zp, :, n], r3b.at[z, :, n], r3_send.at[half, d - 1], r3_recv.at[half, d - 1], at_z(zp))]

    def go(step, half):
        for d in (1, 2, 3):
            for c in step(half, d):
                c.start()

    def got(step, half):
        for d in (1, 2, 3):
            for c in step(half, d):
                c.wait_recv()

    def r1_finish(half):
        got(r1, half)
        for i in (0, 1):
            for first in range(0, HALF, 512):
                n = pl.ds(half * HALF + first, 512)
                terms = dot(sel_ref[i], dlisted[i, :, :, n].reshape(4 * FAR, 512), TN)
                r2s[i, :, :, n] = terms.astype(BF16).reshape(4, 16, 512)
        go(r2, half)

    def r2_finish(half):
        n = half_lanes(half)
        got(r2, half)
        for j, c in enumerate((x, y)):
            total = r2s[j, c, :, n].astype(F32)
            for d in (1, 2, 3):
                total = total + r2b[j, behind(c, d), :, n].astype(F32)
            col32[:, n] = total
            for i in range(4):
                r3s[i, 4 * j : 4 * j + 4, n] = col32[4 * i : 4 * i + 4, n]
        go(r3, half)

    def r3_finish(half):
        n = half_lanes(half)
        got(r3, half)
        total = r3s[z, :, n]
        for d in (1, 2, 3):
            total = total + r3b[behind(z, d), :, n]
        far_grad[:, n] = total * (1.0 / 128)

    def outs(p):
        return [
            pltpu.make_async_copy(ox.at[p], o_hbm.at[:, cols(p)], out_sem.at[p, 0]),
            pltpu.make_async_copy(dqx.at[p], dq_hbm.at[:, cols(p)], out_sem.at[p, 1]),
            pltpu.make_async_copy(qx.at[p], dk_hbm.at[:, cols(p)], out_sem.at[p, 2]),
            pltpu.make_async_copy(gx.at[p], dv_hbm.at[:, cols(p)], out_sem.at[p, 3]),
        ]

    @pl.loop(0, PAIRS)
    def _(p):
        for i, dst in enumerate((kx, vx)):
            rows = listed[i, :, :, cols(p)].astype(F32)
            dst[p, NEAR:LIST, :] = ((rows[0] + rows[1]) + (rows[2] + rows[3])).astype(BF16)
        for c in load(p)[2:]:
            c.wait()
        for c in rims(p):
            c.wait_recv()
        first = head(p, 0)
        second = head(p, 1)
        send_out(p, True)
        for c in outs(p)[:2]:
            c.start()
        for i, slot in ((0, y), (1, x)):
            dlisted[i, slot, :, cols(p)] = jnp.concatenate([first[i], second[i]], axis=1).astype(BF16)

        @pl.when(p < PAIRS - 3)
        def _():
            relay(p + 3, False)

        @pl.when(p >= 2)
        def _():
            relay(p - 2, True)

        @pl.when(p == 3)
        def _():
            go(r1, 0)

        @pl.when(p == 6)
        def _():
            r1_finish(0)

        @pl.when(p == 7)
        def _():
            r2_finish(0)

    go(r1, 1)
    for p in (PAIRS - 2, PAIRS - 1):
        relay(p, True)

    level_no = lax.broadcasted_iota(jnp.int32, (8, FAR), 0)
    list_row = lax.broadcasted_iota(jnp.int32, (8, FAR), 1)
    level_of = jnp.where(list_row < 16, 0, jnp.where(list_row < 24, 1, jnp.where(list_row < 28, 2, 9)))
    pick = jnp.where(level_no == level_of, 1.0, 0.0).astype(F32)
    lvy[y] = lax.dot_general(pick, lvl[...], NN, precision=lax.Precision.HIGHEST, preferred_element_type=F32)

    def level_copy(buf, c, step, d, to):
        return remote(buf.at[c], buf.at[c], l_send.at[step, d - 1], l_recv.at[step, d - 1], to)

    def level_steps(step):
        buf, c, at = ((lvy, y, at_y), (lvx, x, at_x), (lvz, z, at_z))[step]
        return [level_copy(buf, c, step, d, at(ahead(c, d))) for d in (1, 2, 3)]

    def level_sum(step):
        for c in level_steps(step):
            c.wait_recv()
        buf = (lvy, lvx, lvz)[step]
        return (buf[0] + buf[1]) + (buf[2] + buf[3])

    for c in level_steps(0):
        c.start()

    def settle(p):
        for c in back(p):
            c.wait_recv()
        for i, dst in enumerate((qx, gx)):
            for r in range(4):
                tokens = pl.ds(128 * r, 128)
                total = own[p, i, tokens, :] + far_grad[4 * i + r : 4 * i + r + 1, cols(p)]
                if r < 2:
                    total = total + from_down[p, i, tokens, :].astype(F32)
                else:
                    total = total + from_up[p, i, pl.ds(128 * (r - 2), 128), :].astype(F32)
                dst[p, tokens, :] = total.astype(BF16)
        for c in outs(p)[2:]:
            c.start()

    r3_finish(0)

    @pl.loop(0, 4)
    def _(p):
        settle(p)

    lvx[x] = level_sum(0)
    for c in level_steps(1):
        c.start()
    r1_finish(1)
    lvz[z] = level_sum(1)
    for c in level_steps(2):
        c.start()
    r2_finish(1)
    lvc[core] = level_sum(2)
    swap = pltpu.make_async_remote_copy(
        src_ref=lvc.at[core], dst_ref=lvc.at[core], send_sem=c_send, recv_sem=c_recv,
        device_id={"batch": 1 - core}, device_id_type=MESH)
    swap.start()
    r3_finish(1)

    @pl.loop(4, PAIRS)
    def _(p):
        settle(p)

    swap.wait_recv()
    level_ref[...] = ((lvc[0] + lvc[1]) * (1.0 / math.sqrt(2 * BLOCKS * LEAF)))[0:3, 0:HEADS]

    swap.wait_send()
    for step in range(3):
        for c in level_steps(step):
            c.wait_send()
    for d in (1, 2, 3):
        gather_z(d).wait_send()
        for c in gather_one(d) + gather_two(d):
            c.wait_send()
        for half in (0, 1):
            for c in r1(half, d) + r2(half, d) + r3(half, d):
                c.wait_send()

    @pl.loop(0, PAIRS)
    def _(p):
        for c in rims(p) + back(p):
            c.wait_send()
        for c in outs(p):
            c.wait()

        @pl.when((z == 0) | (z == 3))
        def _():
            onward(p, False)[0].wait_send()
            onward(p, True)[0].wait_send()


def shards(queries, key_vectors, values, out_grad, far_lists, level_bias):
    any_spec = pl.BlockSpec(memory_space=pl.ANY)
    smem = pl.BlockSpec(memory_space=pltpu.SMEM)
    dma = pltpu.SemaphoreType.DMA
    outs = pl.pallas_call(
        kernel,
        out_shape=[jax.ShapeDtypeStruct((LEAF, WIDTH), BF16)] * 4 + [jax.ShapeDtypeStruct((3, HEADS), F32)],
        in_specs=[any_spec] * 4 + [smem] * 2,
        out_specs=[any_spec] * 4 + [pl.BlockSpec(memory_space=pltpu.VMEM)],
        scratch_shapes=[
            pltpu.VMEM((PAIRS, LIST, PAIR), BF16),
            pltpu.VMEM((PAIRS, LIST, PAIR), BF16),
            pltpu.VMEM((PAIRS, LEAF, PAIR), BF16),
            pltpu.VMEM((PAIRS, LEAF, PAIR), BF16),
            pltpu.VMEM((PAIRS, LEAF, PAIR), BF16),
            pltpu.VMEM((PAIRS, LEAF, PAIR), BF16),
            pltpu.VMEM((PAIRS, 2, LEAF, PAIR), F32),
            pltpu.VMEM((PAIRS, 2, RIM, PAIR), BF16),
            pltpu.VMEM((PAIRS, 2, RIM, PAIR), BF16),
            pltpu.VMEM((PAIRS, 2, RIM, PAIR), BF16),
            pltpu.VMEM((PAIRS, 2, RIM, PAIR), BF16),
            pltpu.VMEM((2, 4, 16, WIDTH), BF16),
            pltpu.VMEM((2, 4, FAR, WIDTH), BF16),
            pltpu.VMEM((2, 4, FAR, WIDTH), BF16),
            pltpu.VMEM((2, 4, FAR, WIDTH), BF16),
            pltpu.VMEM((4, 8, WIDTH), F32),
            pltpu.VMEM((16, WIDTH), F32),
            pltpu.VMEM((2, 4, 16, WIDTH), BF16),
            pltpu.VMEM((2, 4, 16, WIDTH), BF16),
            pltpu.VMEM((4, 8, WIDTH), F32),
            pltpu.VMEM((4, 8, WIDTH), F32),
            pltpu.VMEM((8, WIDTH), F32),
            pltpu.VMEM((2, 4 * FAR, 64), BF16),
            pltpu.VMEM((FAR, 128), F32),
            pltpu.VMEM((4, 8, 128), F32),
            pltpu.VMEM((4, 8, 128), F32),
            pltpu.VMEM((4, 8, 128), F32),
            pltpu.VMEM((2, 8, 128), F32),
            pltpu.VMEM((2, LIST, LEAF), F32),
            pltpu.VMEM((2, LIST, LEAF), BF16),
            pltpu.VMEM((2, LIST, LEAF), BF16),
            pltpu.VMEM((PAIRS, RIM, PAIR), BF16),
            pltpu.VMEM((PAIRS, RIM, PAIR), BF16),
            dma((PAIRS, 2)), dma((PAIRS, 2)),
            dma((PAIRS, 2, 2)), dma((PAIRS, 2, 2)), dma((PAIRS, 2, 2)), dma((PAIRS, 2, 2)),
            dma((PAIRS, 4)), dma((PAIRS, 4)),
            dma((3,)), dma((3,)), dma((2, 3)), dma((2, 3)), dma((2, 3)), dma((2, 3)),
            dma((2, 2, 3)), dma((2, 2, 3)), dma((2, 2, 3)), dma((2, 2, 3)), dma((2, 3)), dma((2, 3)),
            dma((3, 3)), dma((3, 3)), dma, dma,
        ],
        compiler_params=pltpu.CompilerParams(
            collective_id=0, has_side_effects=True, vmem_limit_bytes=62 * 1024 * 1024),
        cost_estimate=pl.CostEstimate(
            flops=12 * HEADS * LEAF * LIST * DIM, bytes_accessed=8 * LEAF * WIDTH * 2,
            transcendentals=HEADS * LEAF * LIST),
    )(queries[0], key_vectors[0], values[0], out_grad[0], far_lists[0], level_bias)
    return tuple(o[None] for o in outs[:4]) + (outs[4],)


def solution(mesh):
    token = P("batch", "seq", None)
    return jax.shard_map(
        shards,
        mesh=mesh,
        in_specs=(token, token, token, token, P("batch", None, None), P()),
        out_specs=(token, token, token, token, P()),
        check_vma=False,
    )
```

```python
import functools
import math

import jax
import jax.numpy as jnp
from jax import lax
from jax.experimental import pallas as pl
from jax.experimental.pallas import tpu as pltpu
from jax.sharding import PartitionSpec as P

HEADS = 16
DIM = 128
WIDTH = HEADS * DIM
LEAF = 512
RIM = 256
BLOCKS = 64
PAIRS = 8
PAIR = 2 * DIM
NEAR = LEAF + 2 * RIM
FAR = 32
LIST = NEAR + FAR
SCALE = 1.0 / math.sqrt(DIM)
LOG2E = math.log2(math.e)
BIG = 1e30
MESH = pl.DeviceIdType.MESH
F32 = jnp.float32
BF16 = jnp.bfloat16
PARTS = ((0, 6 * PAIR), (6 * PAIR, 2 * PAIR))

DIRECT, SPLIT, RELAY = (False, False), (False, True), (True, True)
FWD_ROUTE = (SPLIT,) * PAIRS
BWD_ROUTE = (SPLIT,) * PAIRS
PROLOGUE = ((("f", 0),), (), tuple(("f", p) for p in range(1, PAIRS)), (("rf", 0),), (("rf", 1), ("rf", 2)))
BEFORE = ((),) * PAIRS
AFTER = (
    (("b", 0), ("rf", 3)),
    (("b", 1), ("rf", 4)),
    (("b", 2), ("rf", 5), ("rb", 0)),
    (("b", 3), ("rf", 6), ("rb", 1)),
    (("b", 4), ("rf", 7), ("rb", 2)),
    (("b", 5), ("rb", 3), ("x", 0)),
    (("b", 6), ("rb", 4)),
    (("b", 7), ("rb", 5), ("y", 0)),
)
TAIL = (
    ("x", 1), ("l", 0), ("w", 0), ("y", 1), ("l", 1), ("v", 0), ("rb", 6), ("s", 0), ("s", 1), ("s", 2), ("s", 3),
    ("w", 1), ("l", 2), ("rb", 7), ("s", 4), ("s", 5), ("l", 3), ("v", 1), ("s", 6), ("s", 7),
)

NT = (((1,), (1,)), ((), ()))
TN = (((0,), (0,)), ((), ()))
NN = (((1,), (0,)), ((), ()))

CHUNKS = ((0, 256), (256, 256), (512, 256), (768, 256), (1024, FAR))


def dot(a, b, dims=NN):
    return lax.dot_general(a, b, dims, preferred_element_type=F32)


def selector(lists_ref, reader, block):
    shape = (FAR, 64)
    row = lax.broadcasted_iota(jnp.int32, shape, 0)
    col = lax.broadcasted_iota(jnp.int32, shape, 1)
    wanted = jnp.full(shape, -1, jnp.int32)
    first = 0
    for level, count in enumerate((4, 2, 1)):
        for slot in range(4):
            listed = lists_ref[level * 4 + slot, 0, reader]
            wanted = jnp.where((row >= first) & (row < first + count), listed, wanted)
            first += count
    part = col & 3
    one = (row < 16) & (part == (row & 3))
    two = (row >= 16) & (row < 24) & ((part >> 1) == (row & 1))
    share = jnp.where(one, 1.0, 0.0) + jnp.where(two, 0.5, 0.0) + jnp.where(row >= 24, 0.25, 0.0)
    return jnp.where(wanted == block, share, 0.0).astype(BF16)


def kernel(
    q_hbm, k_hbm, v_hbm, g_hbm, lists_ref, bias_ref,
    o_ref, dq_ref, dk_ref, dv_ref, level_ref,
    kx, vx, qx, gx, own, to_down, to_up, from_up, from_down,
    table, chosen, listed, dlisted, zbuf, col32, r2s, r2b, r3s, r3b, far_grad,
    sel_ref, lvl, lvz, lvx, lvy, lvc, s_ref, w_ref, d_ref,
    fwd_relay, bwd_relay, relay_send, relay_recv,
    fwd_send, fwd_recv, bwd_send, bwd_recv, in_sem,
    z_send, z_recv, a1_send, a1_recv, a2_send, a2_recv,
    r1_send, r1_recv, r2_send, r2_recv, r3_send, r3_recv,
    l_send, l_recv, c_send, c_recv,
):
    me = lax.axis_index("seq")
    core = lax.axis_index("batch")
    z = lax.rem(me, 4)
    x = lax.rem(lax.div(me, 4), 4)
    y = lax.div(me, 16)
    up = lax.rem(me + 1, BLOCKS)
    down = lax.rem(me + BLOCKS - 1, BLOCKS)
    next_z = lax.rem(me + 4, BLOCKS)
    last_z = lax.rem(me + BLOCKS - 4, BLOCKS)

    def ahead(c, d):
        return lax.rem(c + d, 4)

    def behind(c, d):
        return lax.rem(c + 4 - d, 4)

    def at_y(c):
        return c * 16 + x * 4 + z

    def at_x(c):
        return y * 16 + c * 4 + z

    def at_z(c):
        return y * 16 + x * 4 + c

    def remote(src, dst, send, recv, to):
        return pltpu.make_async_remote_copy(
            src_ref=src, dst_ref=dst, send_sem=send, recv_sem=recv,
            device_id={"seq": to}, device_id_type=MESH,
        )

    barrier = pltpu.get_barrier_semaphore()
    partners = [up, down, next_z, last_z]
    for d in (1, 2, 3):
        partners += [at_z(ahead(z, d)), at_x(ahead(x, d)), at_y(ahead(y, d))]
    for to in partners:
        pl.semaphore_signal(barrier, inc=1, device_id={"seq": to}, device_id_type=MESH)
    pl.semaphore_signal(barrier, inc=1, device_id={"batch": 1 - core}, device_id_type=MESH)

    def cols(p):
        return pl.ds(pl.multiple_of(p * PAIR, PAIR), PAIR)

    def load(p):
        return [
            pltpu.make_async_copy(k_hbm.at[:, cols(p)], kx.at[p, pl.ds(RIM, LEAF), :], in_sem.at[p, 0]),
            pltpu.make_async_copy(v_hbm.at[:, cols(p)], vx.at[p, pl.ds(RIM, LEAF), :], in_sem.at[p, 1]),
            pltpu.make_async_copy(q_hbm.at[:, cols(p)], qx.at[p], in_sem.at[p, 2]),
            pltpu.make_async_copy(g_hbm.at[:, cols(p)], gx.at[p], in_sem.at[p, 3]),
        ]

    low_rim, high_rim = pl.ds(0, RIM), pl.ds(RIM + LEAF, RIM)

    def rims(p):
        lower, upper = pl.ds(0, RIM), pl.ds(RIM, RIM)
        found = []
        for i, (src, dst) in enumerate(((k_hbm, kx), (v_hbm, vx))):
            found.append(remote(src.at[upper, cols(p)], dst.at[p, low_rim, :], fwd_send.at[p, i, 0], fwd_recv.at[p, i, 0], up))
            found.append(remote(src.at[lower, cols(p)], dst.at[p, high_rim, :], fwd_send.at[p, i, 1], fwd_recv.at[p, i, 1], down))
        return found

    def back(p):
        found = []
        for i in (0, 1):
            found.append(remote(to_up.at[p, i], from_down.at[p, i], bwd_send.at[p, i, 0], bwd_recv.at[p, i, 0], up))
            found.append(remote(to_down.at[p, i], from_up.at[p, i], bwd_send.at[p, i, 1], bwd_recv.at[p, i, 1], down))
        return found

    def detour(p, i, backward):
        if backward:
            up_part, down_part, held, send = to_up.at[p, i], to_down.at[p, i], bwd_relay.at[p, i], bwd_send
        else:
            src = (k_hbm, v_hbm)[i]
            up_part, down_part = src.at[pl.ds(RIM, RIM), cols(p)], src.at[pl.ds(0, RIM), cols(p)]
            held, send = fwd_relay.at[p, i], fwd_send
        recv = relay_recv.at[backward, p, i]
        return (remote(up_part, held, send.at[p, i, 0], recv, at_z(0)),
                remote(down_part, held, send.at[p, i, 1], recv, at_z(3)))

    def onward(p, i, backward):
        send = relay_send.at[backward, p, i]
        if backward:
            held, recv, ups, downs = bwd_relay.at[p, i], bwd_recv, from_down.at[p, i], from_up.at[p, i]
        else:
            dst = (kx, vx)[i]
            held, recv, ups, downs = fwd_relay.at[p, i], fwd_recv, dst.at[p, low_rim, :], dst.at[p, high_rim, :]
        return (remote(held, ups, send, recv.at[p, i, 0], next_z),
                remote(held, downs, send, recv.at[p, i, 1], last_z))

    def start_when(condition, copy):
        @pl.when(condition)
        def _():
            copy.start()

    def send_out(p, backward):
        copies = back(p) if backward else rims(p)
        for i in (0, 1):
            part_up, part_down = copies[2 * i : 2 * i + 2]
            if (FWD_ROUTE, BWD_ROUTE)[backward][p][i]:
                far_up, far_down = detour(p, i, backward)
                start_when(z != 3, part_up)
                start_when(z == 3, far_up)
                start_when(z != 0, part_down)
                start_when(z == 0, far_down)
            else:
                part_up.start()
                part_down.start()

    def relay(p, backward):
        for i in (0, 1):
            if (FWD_ROUTE, BWD_ROUTE)[backward][p][i]:
                for place, came, on in zip((0, 3), detour(p, i, backward), onward(p, i, backward)):
                    @pl.when(z == place)
                    def _():
                        came.wait_recv()
                        on.start()

    def part_lanes(part):
        return pl.ds(*PARTS[part])

    def r1(part, d):
        n = part_lanes(part)
        yp, xp = ahead(y, d), ahead(x, d)
        return [
            remote(dlisted.at[0, y, :, n], dlisted.at[0, y, :, n], r1_send.at[part, 0, d - 1], r1_recv.at[part, 0, d - 1], at_y(yp)),
            remote(dlisted.at[1, x, :, n], dlisted.at[1, x, :, n], r1_send.at[part, 1, d - 1], r1_recv.at[part, 1, d - 1], at_x(xp)),
        ]

    def r2(part, d):
        n = part_lanes(part)
        yp, xp = ahead(y, d), ahead(x, d)
        return [
            remote(r2s.at[0, xp, :, n], r2b.at[0, x, :, n], r2_send.at[part, 0, d - 1], r2_recv.at[part, 0, d - 1], at_x(xp)),
            remote(r2s.at[1, yp, :, n], r2b.at[1, y, :, n], r2_send.at[part, 1, d - 1], r2_recv.at[part, 1, d - 1], at_y(yp)),
        ]

    def r3(part, d):
        n = part_lanes(part)
        zp = ahead(z, d)
        return [remote(r3s.at[zp, :, n], r3b.at[z, :, n], r3_send.at[part, d - 1], r3_recv.at[part, d - 1], at_z(zp))]

    def go(step, part):
        for d in (1, 2, 3):
            for c in step(part, d):
                c.start()

    def got(step, part):
        for d in (1, 2, 3):
            for c in step(part, d):
                c.wait_recv()

    def r1_finish(part):
        got(r1, part)
        for i in (0, 1):
            for first in range(0, PARTS[part][1], 512):
                n = pl.ds(PARTS[part][0] + first, 512)
                terms = dot(sel_ref[i], dlisted[i, :, :, n].reshape(4 * FAR, 512), TN)
                r2s[i, :, :, n] = terms.astype(BF16).reshape(4, 16, 512)
        go(r2, part)

    def r2_finish(part):
        n = part_lanes(part)
        got(r2, part)
        for j, c in enumerate((x, y)):
            total = r2s[j, c, :, n].astype(F32)
            for d in (1, 2, 3):
                total = total + r2b[j, behind(c, d), :, n].astype(F32)
            col32[:, n] = total
            for i in range(4):
                r3s[i, 4 * j : 4 * j + 4, n] = col32[4 * i : 4 * i + 4, n]
        go(r3, part)

    def r3_finish(part):
        n = part_lanes(part)
        got(r3, part)
        total = r3s[z, :, n]
        for d in (1, 2, 3):
            total = total + r3b[behind(z, d), :, n]
        far_grad[:, n] = total * (1.0 / 128)

    swap = pltpu.make_async_remote_copy(
        src_ref=lvc.at[core], dst_ref=lvc.at[core], send_sem=c_send, recv_sem=c_recv,
        device_id={"batch": 1 - core}, device_id_type=MESH)

    def level_copy(buf, c, step, d, to):
        return remote(buf.at[c], buf.at[c], l_send.at[step, d - 1], l_recv.at[step, d - 1], to)

    def level_steps(step):
        buf, c, at = ((lvy, y, at_y), (lvx, x, at_x), (lvz, z, at_z))[step]
        return [level_copy(buf, c, step, d, at(ahead(c, d))) for d in (1, 2, 3)]

    def level_sum(step):
        for c in level_steps(step):
            c.wait_recv()
        buf = (lvy, lvx, lvz)[step]
        return (buf[0] + buf[1]) + (buf[2] + buf[3])

    def level_step(n):
        if n == 0:
            level_no = lax.broadcasted_iota(jnp.int32, (8, FAR), 0)
            list_row = lax.broadcasted_iota(jnp.int32, (8, FAR), 1)
            level_of = jnp.where(list_row < 16, 0, jnp.where(list_row < 24, 1, jnp.where(list_row < 28, 2, 9)))
            pick = jnp.where(level_no == level_of, 1.0, 0.0).astype(F32)
            lvy[y] = lax.dot_general(pick, lvl[...], NN, precision=lax.Precision.HIGHEST, preferred_element_type=F32)
        else:
            buf, c = ((lvx, x), (lvz, z), (lvc, core))[n - 1]
            buf[c] = level_sum(n - 1)
        for c in level_steps(n) if n < 3 else [swap]:
            c.start()

    def settle(p):
        for c in back(p):
            c.wait_recv()
        for i, dst in enumerate((dk_ref, dv_ref)):
            for r in range(4):
                tokens = pl.ds(128 * r, 128)
                total = own[p, i, tokens, :] + far_grad[4 * i + r : 4 * i + r + 1, cols(p)]
                if r < 2:
                    total = total + from_down[p, i, tokens, :].astype(F32)
                else:
                    total = total + from_up[p, i, pl.ds(128 * (r - 2), 128), :].astype(F32)
                dst[tokens, cols(p)] = total.astype(BF16)

    def act(steps):
        for kind, n in steps:
            if kind in ("f", "b"):
                send_out(n, ("f", "b").index(kind))
            elif kind in ("rf", "rb"):
                relay(n, ("rf", "rb").index(kind))
            elif kind == "x":
                go(r1, n)
            else:
                {"y": r1_finish, "w": r2_finish, "v": r3_finish, "s": settle, "l": level_step}[kind](n)

    @pl.loop(0, PAIRS)
    def _(p):
        for c in load(p)[:2]:
            c.start()

    @pl.loop(0, PAIRS)
    def _(p):
        for c in load(p)[2:]:
            c.start()

    pl.semaphore_wait(barrier, 14)
    act(PROLOGUE[0])

    col_block = lax.broadcasted_iota(jnp.int32, (FAR, 64), 1) // 4
    key_block = y * 16 + col_block
    value_block = (col_block // 4) * 16 + x * 4 + (col_block & 3)
    for i in range(4):
        sel_ref[0, i * FAR : (i + 1) * FAR, :] = selector(lists_ref, at_y(i), key_block)
        sel_ref[1, i * FAR : (i + 1) * FAR, :] = selector(lists_ref, at_x(i), value_block)

    pool_row = lax.broadcasted_iota(jnp.int32, (8, LEAF), 0)
    pool_tok = lax.broadcasted_iota(jnp.int32, (8, LEAF), 1) // 128
    pool_k = jnp.where(pool_tok == pool_row, 1.0 / 128, 0.0).astype(BF16)
    pool_v = jnp.where(pool_tok + 4 == pool_row, 1.0 / 128, 0.0).astype(BF16)

    @pl.loop(0, PAIRS)
    def _(p):
        for c in load(p)[:2]:
            c.wait()
        mine = pl.ds(RIM, LEAF)
        zbuf[z, :, cols(p)] = dot(pool_k, kx[p, mine, :]) + dot(pool_v, vx[p, mine, :])

    def gather_z(d):
        return remote(zbuf.at[z], zbuf.at[z], z_send.at[d - 1], z_recv.at[d - 1], at_z(ahead(z, d)))

    for d in (1, 2, 3):
        gather_z(d).start()
    act(PROLOGUE[1])
    for d in (1, 2, 3):
        gather_z(d).wait_recv()
    for i in (0, 1):
        for c in range(4):
            col32[4 * c : 4 * c + 4, :] = zbuf[c, 4 * i : 4 * i + 4, :]
        table[i, (x, y)[i]] = col32[...].astype(BF16)

    def gather_one(d):
        return [
            remote(table.at[0, x], table.at[0, x], a1_send.at[0, d - 1], a1_recv.at[0, d - 1], at_x(ahead(x, d))),
            remote(table.at[1, y], table.at[1, y], a1_send.at[1, d - 1], a1_recv.at[1, d - 1], at_y(ahead(y, d))),
        ]

    def gather_two(d):
        yp, xp = ahead(y, d), ahead(x, d)
        return [
            remote(chosen.at[0, yp], listed.at[0, y], a2_send.at[0, d - 1], a2_recv.at[0, d - 1], at_y(yp)),
            remote(chosen.at[1, xp], listed.at[1, x], a2_send.at[1, d - 1], a2_recv.at[1, d - 1], at_x(xp)),
        ]

    for d in (1, 2, 3):
        for c in gather_one(d):
            c.start()
    act(PROLOGUE[2])
    for d in (1, 2, 3):
        for c in gather_one(d):
            c.wait_recv()
    for i in (0, 1):
        for n in range(0, WIDTH, 512):
            rows = table[i, :, :, n : n + 512].reshape(64, 512)
            chosen[i, :, :, n : n + 512] = dot(sel_ref[i], rows).astype(BF16).reshape(4, FAR, 512)
    for d in (1, 2, 3):
        for c in gather_two(d):
            c.start()
    listed[0, y] = chosen[0, y]
    listed[1, x] = chosen[1, x]

    act(PROLOGUE[3])
    for d in (1, 2, 3):
        for c in gather_two(d):
            c.wait_recv()
    act(PROLOGUE[4])

    lane_sel = lax.broadcasted_iota(jnp.int32, (FAR, 128), 1)
    far_row = lax.broadcasted_iota(jnp.int32, (FAR, 1), 0)
    lvl[...] = jnp.zeros_like(lvl)
    low_gap = jnp.where(me == 0, BIG, 0.0).astype(F32)
    high_gap = jnp.where(me == BLOCKS - 1, BIG, 0.0).astype(F32)
    gaps = (low_gap, None, None, high_gap, None)
    factor = SCALE * LOG2E

    def head(p, h):
        lanes = slice(h * DIM, h * DIM + DIM)
        head_no = 2 * p + h
        head_lanes = pl.ds(pl.multiple_of(head_no * DIM, DIM), DIM)
        bias = jnp.where(
            far_row < 16, bias_ref[0, head_no] + math.log(128),
            jnp.where(far_row < 24, bias_ref[1, head_no] + math.log(256),
                      jnp.where(far_row < 28, bias_ref[2, head_no] + math.log(512), -BIG)))
        bias = bias * LOG2E
        query = qx[p, :, lanes]
        grad = gx[p, :, lanes]
        top = None
        for (first, rows), gap in zip(CHUNKS, gaps):
            s = dot(kx[p, first : first + rows, lanes], query, NT) * factor
            if rows == FAR:
                s = s + bias
            s_ref[h, first : first + rows, :] = s
            peak = jnp.max(s, axis=0, keepdims=True)
            if gap is not None:
                peak = peak - gap
            top = peak if top is None else jnp.maximum(top, peak)
        total = jnp.zeros((1, LEAF), F32)
        for (first, rows), gap in zip(CHUNKS, gaps):
            base = top if gap is None else top + gap
            e = jnp.exp2(s_ref[h, first : first + rows, :] - base)
            s_ref[h, first : first + rows, :] = e
            total = total + jnp.sum(e, axis=0, keepdims=True)
        inverse = 1.0 / total
        for first, rows in CHUNKS:
            w_ref[h, first : first + rows, :] = (s_ref[h, first : first + rows, :] * inverse).astype(BF16)
        out = dot(vx[p, :, lanes], w_ref[h], TN).T.astype(BF16)
        o_ref[:, head_lanes] = out
        ones = jnp.ones((8, DIM), F32)
        row_dot = lax.dot_general(
            ones, out.astype(F32) * grad.astype(F32), NT,
            precision=lax.Precision.HIGHEST, preferred_element_type=F32)[0:1, :]
        for first, rows in CHUNKS:
            dw = dot(vx[p, first : first + rows, lanes], grad, NT)
            ds = s_ref[h, first : first + rows, :] * inverse * (dw - row_dot)
            d_ref[h, first : first + rows, :] = ds.astype(BF16)
            if rows == FAR:
                sums = jnp.sum(ds, axis=1, keepdims=True)
                lvl[...] += jnp.where(lane_sel == head_no, sums, 0.0)
        dq_ref[:, head_lanes] = (dot(kx[p, :, lanes], d_ref[h], TN) * SCALE).T.astype(BF16)
        dk = dot(d_ref[h], query) * SCALE
        dv = dot(w_ref[h], grad)
        for i, term in enumerate((dk, dv)):
            to_down[p, i, :, lanes] = term[:RIM].astype(BF16)
            own[p, i, :, lanes] = term[RIM : RIM + LEAF]
            to_up[p, i, :, lanes] = term[RIM + LEAF : NEAR].astype(BF16)
        return dk[NEAR:], dv[NEAR:]

    @pl.loop(0, PAIRS)
    def _(p):
        for i, dst in enumerate((kx, vx)):
            rows = listed[i, :, :, cols(p)].astype(F32)
            dst[p, NEAR:LIST, :] = ((rows[0] + rows[1]) + (rows[2] + rows[3])).astype(BF16)
        for c in load(p)[2:]:
            c.wait()
        for c in rims(p):
            c.wait_recv()

        def at_step(k, steps):
            if steps:
                @pl.when(p == k)
                def _():
                    act(steps)

        for k in range(PAIRS):
            at_step(k, BEFORE[k])
        first = head(p, 0)
        second = head(p, 1)
        for i, slot in ((0, y), (1, x)):
            dlisted[i, slot, :, cols(p)] = jnp.concatenate([first[i], second[i]], axis=1).astype(BF16)

        for k in range(PAIRS):
            at_step(k, AFTER[k])

    act(TAIL)

    swap.wait_recv()
    level_ref[...] = ((lvc[0] + lvc[1]) * (1.0 / math.sqrt(2 * BLOCKS * LEAF)))[0:3, 0:HEADS]

    swap.wait_send()
    for step in range(3):
        for c in level_steps(step):
            c.wait_send()
    for d in (1, 2, 3):
        gather_z(d).wait_send()
        for c in gather_one(d) + gather_two(d):
            c.wait_send()
        for part in (0, 1):
            for c in r1(part, d) + r2(part, d) + r3(part, d):
                c.wait_send()

    @pl.loop(0, PAIRS)
    def _(p):
        for c in rims(p) + back(p):
            c.wait_send()

    @pl.when((z == 0) | (z == 3))
    def _():
        for backward in (0, 1):
            for p in range(PAIRS):
                for i in (0, 1):
                    if (FWD_ROUTE, BWD_ROUTE)[backward][p][i]:
                        onward(p, i, backward)[0].wait_send()


def shards(queries, key_vectors, values, out_grad, far_lists, level_bias):
    any_spec = pl.BlockSpec(memory_space=pl.ANY)
    smem = pl.BlockSpec(memory_space=pltpu.SMEM)
    dma = pltpu.SemaphoreType.DMA
    outs = pl.pallas_call(
        kernel,
        out_shape=[pltpu.VMEM((LEAF, WIDTH), BF16)] * 4 + [pltpu.VMEM((3, HEADS), F32)],
        in_specs=[any_spec] * 4 + [smem] * 2,
        out_specs=[pl.BlockSpec(memory_space=pltpu.VMEM)] * 4 + [pl.BlockSpec(memory_space=pltpu.VMEM)],
        scratch_shapes=[
            pltpu.VMEM((PAIRS, LIST, PAIR), BF16),
            pltpu.VMEM((PAIRS, LIST, PAIR), BF16),
            pltpu.VMEM((PAIRS, LEAF, PAIR), BF16),
            pltpu.VMEM((PAIRS, LEAF, PAIR), BF16),
            pltpu.VMEM((PAIRS, 2, LEAF, PAIR), F32),
            pltpu.VMEM((PAIRS, 2, RIM, PAIR), BF16),
            pltpu.VMEM((PAIRS, 2, RIM, PAIR), BF16),
            pltpu.VMEM((PAIRS, 2, RIM, PAIR), BF16),
            pltpu.VMEM((PAIRS, 2, RIM, PAIR), BF16),
            pltpu.VMEM((2, 4, 16, WIDTH), BF16),
            pltpu.VMEM((2, 4, FAR, WIDTH), BF16),
            pltpu.VMEM((2, 4, FAR, WIDTH), BF16),
            pltpu.VMEM((2, 4, FAR, WIDTH), BF16),
            pltpu.VMEM((4, 8, WIDTH), F32),
            pltpu.VMEM((16, WIDTH), F32),
            pltpu.VMEM((2, 4, 16, WIDTH), BF16),
            pltpu.VMEM((2, 4, 16, WIDTH), BF16),
            pltpu.VMEM((4, 8, WIDTH), F32),
            pltpu.VMEM((4, 8, WIDTH), F32),
            pltpu.VMEM((8, WIDTH), F32),
            pltpu.VMEM((2, 4 * FAR, 64), BF16),
            pltpu.VMEM((FAR, 128), F32),
            pltpu.VMEM((4, 8, 128), F32),
            pltpu.VMEM((4, 8, 128), F32),
            pltpu.VMEM((4, 8, 128), F32),
            pltpu.VMEM((2, 8, 128), F32),
            pltpu.VMEM((2, LIST, LEAF), F32),
            pltpu.VMEM((2, LIST, LEAF), BF16),
            pltpu.VMEM((2, LIST, LEAF), BF16),
            pltpu.VMEM((PAIRS, 2, RIM, PAIR), BF16),
            pltpu.VMEM((PAIRS, 2, RIM, PAIR), BF16),
            dma((2, PAIRS, 2)), dma((2, PAIRS, 2)),
            dma((PAIRS, 2, 2)), dma((PAIRS, 2, 2)), dma((PAIRS, 2, 2)), dma((PAIRS, 2, 2)),
            dma((PAIRS, 4)),
            dma((3,)), dma((3,)), dma((2, 3)), dma((2, 3)), dma((2, 3)), dma((2, 3)),
            dma((2, 2, 3)), dma((2, 2, 3)), dma((2, 2, 3)), dma((2, 2, 3)), dma((2, 3)), dma((2, 3)),
            dma((3, 3)), dma((3, 3)), dma, dma,
        ],
        compiler_params=pltpu.CompilerParams(
            collective_id=0, has_side_effects=True, vmem_limit_bytes=54 * 1024 * 1024),
        cost_estimate=pl.CostEstimate(
            flops=12 * HEADS * LEAF * LIST * DIM, bytes_accessed=8 * LEAF * WIDTH * 2,
            transcendentals=HEADS * LEAF * LIST),
    )(queries[0], key_vectors[0], values[0], out_grad[0], far_lists.transpose(2, 0, 1), level_bias)
    return tuple(o[None] for o in outs[:4]) + (outs[4],)


def solution(mesh):
    token = P("batch", "seq", None)
    return jax.shard_map(
        shards,
        mesh=mesh,
        in_specs=(token, token, token, token, P("batch", None, None), P()),
        out_specs=(token, token, token, token, P()),
        check_vma=False,
    )
```

```python
import functools
import math

import jax
import jax.numpy as jnp
from jax import lax
from jax.experimental import pallas as pl
from jax.experimental.pallas import tpu as pltpu
from jax.sharding import PartitionSpec as P

HEADS = 16
DIM = 128
WIDTH = HEADS * DIM
LEAF = 512
RIM = 256
BLOCKS = 64
PAIRS = 8
PAIR = 2 * DIM
NEAR = LEAF + 2 * RIM
FAR = 32
LIST = NEAR + FAR
SCALE = 1.0 / math.sqrt(DIM)
LOG2E = math.log2(math.e)
BIG = 1e30
MESH = pl.DeviceIdType.MESH
F32 = jnp.float32
BF16 = jnp.bfloat16
PARTS = ((0, 6 * PAIR), (6 * PAIR, 2 * PAIR))

DIRECT, SPLIT, RELAY = (False, False), (False, True), (True, True)
FWD_ROUTE = (SPLIT,) * PAIRS
BWD_ROUTE = (SPLIT,) * PAIRS
PROLOGUE = ((("f", 0),), (("f", 1),), tuple(("f", p) for p in range(2, PAIRS)), (("rf", 0),), (("rf", 1), ("rf", 2), ("rf", 3)))
BEFORE = ((),) * PAIRS
AFTER = (
    (("b", 0), ("rf", 4)),
    (("b", 1), ("rf", 5)),
    (("b", 2), ("rf", 6)),
    (("b", 3), ("rf", 7), ("rb", 0)),
    (("b", 4), ("rb", 1)),
    (("b", 5), ("rb", 2), ("x", 0)),
    (("b", 6), ("rb", 3)),
    (("b", 7), ("rb", 4), ("y", 0)),
)
TAIL = (
    ("x", 1), ("l", 0), ("w", 0), ("rb", 5), ("y", 1), ("l", 1), ("v", 0), ("rb", 6), ("s", 0), ("s", 1), ("s", 2), ("s", 3),
    ("w", 1), ("l", 2), ("rb", 7), ("s", 4), ("s", 5), ("l", 3), ("v", 1), ("s", 6), ("s", 7),
)

NT = (((1,), (1,)), ((), ()))
TN = (((0,), (0,)), ((), ()))
NN = (((1,), (0,)), ((), ()))

CHUNKS = ((0, 256), (256, 256), (512, 256), (768, 256), (1024, FAR))


def dot(a, b, dims=NN):
    return lax.dot_general(a, b, dims, preferred_element_type=F32)


def selector(lists_ref, reader, block):
    shape = (FAR, 64)
    row = lax.broadcasted_iota(jnp.int32, shape, 0)
    col = lax.broadcasted_iota(jnp.int32, shape, 1)
    wanted = jnp.full(shape, -1, jnp.int32)
    first = 0
    for level, count in enumerate((4, 2, 1)):
        for slot in range(4):
            listed = lists_ref[level * 4 + slot, 0, reader]
            wanted = jnp.where((row >= first) & (row < first + count), listed, wanted)
            first += count
    part = col & 3
    one = (row < 16) & (part == (row & 3))
    two = (row >= 16) & (row < 24) & ((part >> 1) == (row & 1))
    share = jnp.where(one, 1.0, 0.0) + jnp.where(two, 0.5, 0.0) + jnp.where(row >= 24, 0.25, 0.0)
    return jnp.where(wanted == block, share, 0.0).astype(BF16)


def kernel(
    q_hbm, k_hbm, v_hbm, g_hbm, lists_ref, bias_ref,
    o_ref, dq_ref, dk_ref, dv_ref, level_ref,
    kx, vx, qx, gx, own, to_down, to_up, from_up, from_down,
    table, chosen, listed, dlisted, zbuf, col32, r2s, r2b, r3s, r3b, far_grad,
    sel_ref, lvl, lvz, lvx, lvy, lvc, s_ref, w_ref, d_ref,
    fwd_relay, bwd_relay, relay_send, relay_recv,
    fwd_send, fwd_recv, bwd_send, bwd_recv, in_sem,
    z_send, z_recv, a1_send, a1_recv, a2_send, a2_recv,
    r1_send, r1_recv, r2_send, r2_recv, r3_send, r3_recv,
    l_send, l_recv, c_send, c_recv,
):
    me = lax.axis_index("seq")
    core = lax.axis_index("batch")
    z = lax.rem(me, 4)
    x = lax.rem(lax.div(me, 4), 4)
    y = lax.div(me, 16)
    up = lax.rem(me + 1, BLOCKS)
    down = lax.rem(me + BLOCKS - 1, BLOCKS)
    next_z = lax.rem(me + 4, BLOCKS)
    last_z = lax.rem(me + BLOCKS - 4, BLOCKS)

    def ahead(c, d):
        return lax.rem(c + d, 4)

    def behind(c, d):
        return lax.rem(c + 4 - d, 4)

    def at_y(c):
        return c * 16 + x * 4 + z

    def at_x(c):
        return y * 16 + c * 4 + z

    def at_z(c):
        return y * 16 + x * 4 + c

    def remote(src, dst, send, recv, to):
        return pltpu.make_async_remote_copy(
            src_ref=src, dst_ref=dst, send_sem=send, recv_sem=recv,
            device_id={"seq": to}, device_id_type=MESH,
        )

    barrier = pltpu.get_barrier_semaphore()
    partners = [up, down, next_z, last_z]
    for d in (1, 2, 3):
        partners += [at_z(ahead(z, d)), at_x(ahead(x, d)), at_y(ahead(y, d))]
    for to in partners:
        pl.semaphore_signal(barrier, inc=1, device_id={"seq": to}, device_id_type=MESH)
    pl.semaphore_signal(barrier, inc=1, device_id={"batch": 1 - core}, device_id_type=MESH)

    def cols(p):
        return pl.ds(pl.multiple_of(p * PAIR, PAIR), PAIR)

    def load(p):
        return [
            pltpu.make_async_copy(k_hbm.at[:, cols(p)], kx.at[p, pl.ds(RIM, LEAF), :], in_sem.at[p, 0]),
            pltpu.make_async_copy(v_hbm.at[:, cols(p)], vx.at[p, pl.ds(RIM, LEAF), :], in_sem.at[p, 1]),
            pltpu.make_async_copy(q_hbm.at[:, cols(p)], qx.at[p], in_sem.at[p, 2]),
            pltpu.make_async_copy(g_hbm.at[:, cols(p)], gx.at[p], in_sem.at[p, 3]),
        ]

    low_rim, high_rim = pl.ds(0, RIM), pl.ds(RIM + LEAF, RIM)

    def rims(p):
        lower, upper = pl.ds(0, RIM), pl.ds(RIM, RIM)
        found = []
        for i, (src, dst) in enumerate(((k_hbm, kx), (v_hbm, vx))):
            found.append(remote(src.at[upper, cols(p)], dst.at[p, low_rim, :], fwd_send.at[p, i, 0], fwd_recv.at[p, i, 0], up))
            found.append(remote(src.at[lower, cols(p)], dst.at[p, high_rim, :], fwd_send.at[p, i, 1], fwd_recv.at[p, i, 1], down))
        return found

    def back(p):
        found = []
        for i in (0, 1):
            found.append(remote(to_up.at[p, i], from_down.at[p, i], bwd_send.at[p, i, 0], bwd_recv.at[p, i, 0], up))
            found.append(remote(to_down.at[p, i], from_up.at[p, i], bwd_send.at[p, i, 1], bwd_recv.at[p, i, 1], down))
        return found

    def detour(p, i, backward):
        if backward:
            up_part, down_part, held, send = to_up.at[p, i], to_down.at[p, i], bwd_relay.at[p, i], bwd_send
        else:
            src = (k_hbm, v_hbm)[i]
            up_part, down_part = src.at[pl.ds(RIM, RIM), cols(p)], src.at[pl.ds(0, RIM), cols(p)]
            held, send = fwd_relay.at[p, i], fwd_send
        recv = relay_recv.at[backward, p, i]
        return (remote(up_part, held, send.at[p, i, 0], recv, at_z(0)),
                remote(down_part, held, send.at[p, i, 1], recv, at_z(3)))

    def onward(p, i, backward):
        send = relay_send.at[backward, p, i]
        if backward:
            held, recv, ups, downs = bwd_relay.at[p, i], bwd_recv, from_down.at[p, i], from_up.at[p, i]
        else:
            dst = (kx, vx)[i]
            held, recv, ups, downs = fwd_relay.at[p, i], fwd_recv, dst.at[p, low_rim, :], dst.at[p, high_rim, :]
        return (remote(held, ups, send, recv.at[p, i, 0], next_z),
                remote(held, downs, send, recv.at[p, i, 1], last_z))

    def start_when(condition, copy):
        @pl.when(condition)
        def _():
            copy.start()

    def send_out(p, backward):
        copies = back(p) if backward else rims(p)
        for i in (0, 1):
            part_up, part_down = copies[2 * i : 2 * i + 2]
            if (FWD_ROUTE, BWD_ROUTE)[backward][p][i]:
                far_up, far_down = detour(p, i, backward)
                start_when(z != 3, part_up)
                start_when(z == 3, far_up)
                start_when(z != 0, part_down)
                start_when(z == 0, far_down)
            else:
                part_up.start()
                part_down.start()

    def relay(p, backward):
        for i in (0, 1):
            if (FWD_ROUTE, BWD_ROUTE)[backward][p][i]:
                for place, came, on in zip((0, 3), detour(p, i, backward), onward(p, i, backward)):
                    @pl.when(z == place)
                    def _():
                        came.wait_recv()
                        on.start()

    def part_lanes(part):
        return pl.ds(*PARTS[part])

    def r1(part, d):
        n = part_lanes(part)
        yp, xp = ahead(y, d), ahead(x, d)
        return [
            remote(dlisted.at[0, y, :, n], dlisted.at[0, y, :, n], r1_send.at[part, 0, d - 1], r1_recv.at[part, 0, d - 1], at_y(yp)),
            remote(dlisted.at[1, x, :, n], dlisted.at[1, x, :, n], r1_send.at[part, 1, d - 1], r1_recv.at[part, 1, d - 1], at_x(xp)),
        ]

    def r2(part, d):
        n = part_lanes(part)
        yp, xp = ahead(y, d), ahead(x, d)
        return [
            remote(r2s.at[0, xp, :, n], r2b.at[0, x, :, n], r2_send.at[part, 0, d - 1], r2_recv.at[part, 0, d - 1], at_x(xp)),
            remote(r2s.at[1, yp, :, n], r2b.at[1, y, :, n], r2_send.at[part, 1, d - 1], r2_recv.at[part, 1, d - 1], at_y(yp)),
        ]

    def r3(part, d):
        n = part_lanes(part)
        zp = ahead(z, d)
        return [remote(r3s.at[zp, :, n], r3b.at[z, :, n], r3_send.at[part, d - 1], r3_recv.at[part, d - 1], at_z(zp))]

    def go(step, part):
        for d in (1, 2, 3):
            for c in step(part, d):
                c.start()

    def got(step, part):
        for d in (1, 2, 3):
            for c in step(part, d):
                c.wait_recv()

    def r1_finish(part):
        got(r1, part)
        for i in (0, 1):
            for first in range(0, PARTS[part][1], 512):
                n = pl.ds(PARTS[part][0] + first, 512)
                terms = dot(sel_ref[i], dlisted[i, :, :, n].reshape(4 * FAR, 512), TN)
                r2s[i, :, :, n] = terms.astype(BF16).reshape(4, 16, 512)
        go(r2, part)

    def r2_finish(part):
        n = part_lanes(part)
        got(r2, part)
        for j, c in enumerate((x, y)):
            total = r2s[j, c, :, n].astype(F32)
            for d in (1, 2, 3):
                total = total + r2b[j, behind(c, d), :, n].astype(F32)
            col32[:, n] = total
            for i in range(4):
                r3s[i, 4 * j : 4 * j + 4, n] = col32[4 * i : 4 * i + 4, n]
        go(r3, part)

    def r3_finish(part):
        n = part_lanes(part)
        got(r3, part)
        total = r3s[z, :, n]
        for d in (1, 2, 3):
            total = total + r3b[behind(z, d), :, n]
        far_grad[:, n] = total * (1.0 / 128)

    swap = pltpu.make_async_remote_copy(
        src_ref=lvc.at[core], dst_ref=lvc.at[core], send_sem=c_send, recv_sem=c_recv,
        device_id={"batch": 1 - core}, device_id_type=MESH)

    def level_copy(buf, c, step, d, to):
        return remote(buf.at[c], buf.at[c], l_send.at[step, d - 1], l_recv.at[step, d - 1], to)

    def level_steps(step):
        buf, c, at = ((lvy, y, at_y), (lvx, x, at_x), (lvz, z, at_z))[step]
        return [level_copy(buf, c, step, d, at(ahead(c, d))) for d in (1, 2, 3)]

    def level_sum(step):
        for c in level_steps(step):
            c.wait_recv()
        buf = (lvy, lvx, lvz)[step]
        return (buf[0] + buf[1]) + (buf[2] + buf[3])

    def level_step(n):
        if n == 0:
            level_no = lax.broadcasted_iota(jnp.int32, (8, FAR), 0)
            list_row = lax.broadcasted_iota(jnp.int32, (8, FAR), 1)
            level_of = jnp.where(list_row < 16, 0, jnp.where(list_row < 24, 1, jnp.where(list_row < 28, 2, 9)))
            pick = jnp.where(level_no == level_of, 1.0, 0.0).astype(F32)
            lvy[y] = lax.dot_general(pick, lvl[...], NN, precision=lax.Precision.HIGHEST, preferred_element_type=F32)
        else:
            buf, c = ((lvx, x), (lvz, z), (lvc, core))[n - 1]
            buf[c] = level_sum(n - 1)
        for c in level_steps(n) if n < 3 else [swap]:
            c.start()

    def settle(p):
        for c in back(p):
            c.wait_recv()
        for i, dst in enumerate((dk_ref, dv_ref)):
            for r in range(4):
                tokens = pl.ds(128 * r, 128)
                total = own[p, i, tokens, :] + far_grad[4 * i + r : 4 * i + r + 1, cols(p)]
                if r < 2:
                    total = total + from_down[p, i, tokens, :].astype(F32)
                else:
                    total = total + from_up[p, i, pl.ds(128 * (r - 2), 128), :].astype(F32)
                dst[tokens, cols(p)] = total.astype(BF16)

    def act(steps):
        for kind, n in steps:
            if kind in ("f", "b"):
                send_out(n, ("f", "b").index(kind))
            elif kind in ("rf", "rb"):
                relay(n, ("rf", "rb").index(kind))
            elif kind == "x":
                go(r1, n)
            else:
                {"y": r1_finish, "w": r2_finish, "v": r3_finish, "s": settle, "l": level_step}[kind](n)

    @pl.loop(0, PAIRS)
    def _(p):
        for c in load(p)[:2]:
            c.start()

    @pl.loop(0, PAIRS)
    def _(p):
        for c in load(p)[2:]:
            c.start()

    pl.semaphore_wait(barrier, 14)
    act(PROLOGUE[0])

    col_block = lax.broadcasted_iota(jnp.int32, (FAR, 64), 1) // 4
    key_block = y * 16 + col_block
    value_block = (col_block // 4) * 16 + x * 4 + (col_block & 3)
    for i in range(4):
        sel_ref[0, i * FAR : (i + 1) * FAR, :] = selector(lists_ref, at_y(i), key_block)
        sel_ref[1, i * FAR : (i + 1) * FAR, :] = selector(lists_ref, at_x(i), value_block)

    pool_row = lax.broadcasted_iota(jnp.int32, (8, LEAF), 0)
    pool_tok = lax.broadcasted_iota(jnp.int32, (8, LEAF), 1) // 128
    pool_k = jnp.where(pool_tok == pool_row, 1.0 / 128, 0.0).astype(BF16)
    pool_v = jnp.where(pool_tok + 4 == pool_row, 1.0 / 128, 0.0).astype(BF16)

    @pl.loop(0, PAIRS)
    def _(p):
        for c in load(p)[:2]:
            c.wait()
        mine = pl.ds(RIM, LEAF)
        zbuf[z, :, cols(p)] = dot(pool_k, kx[p, mine, :]) + dot(pool_v, vx[p, mine, :])

    def gather_z(d):
        return remote(zbuf.at[z], zbuf.at[z], z_send.at[d - 1], z_recv.at[d - 1], at_z(ahead(z, d)))

    for d in (1, 2, 3):
        gather_z(d).start()
    act(PROLOGUE[1])
    for d in (1, 2, 3):
        gather_z(d).wait_recv()
    for i in (0, 1):
        for c in range(4):
            col32[4 * c : 4 * c + 4, :] = zbuf[c, 4 * i : 4 * i + 4, :]
        table[i, (x, y)[i]] = col32[...].astype(BF16)

    def gather_one(d):
        return [
            remote(table.at[0, x], table.at[0, x], a1_send.at[0, d - 1], a1_recv.at[0, d - 1], at_x(ahead(x, d))),
            remote(table.at[1, y], table.at[1, y], a1_send.at[1, d - 1], a1_recv.at[1, d - 1], at_y(ahead(y, d))),
        ]

    def gather_two(d):
        yp, xp = ahead(y, d), ahead(x, d)
        return [
            remote(chosen.at[0, yp], listed.at[0, y], a2_send.at[0, d - 1], a2_recv.at[0, d - 1], at_y(yp)),
            remote(chosen.at[1, xp], listed.at[1, x], a2_send.at[1, d - 1], a2_recv.at[1, d - 1], at_x(xp)),
        ]

    for d in (1, 2, 3):
        for c in gather_one(d):
            c.start()
    act(PROLOGUE[2])
    for d in (1, 2, 3):
        for c in gather_one(d):
            c.wait_recv()
    for i in (0, 1):
        for n in range(0, WIDTH, 512):
            rows = table[i, :, :, n : n + 512].reshape(64, 512)
            chosen[i, :, :, n : n + 512] = dot(sel_ref[i], rows).astype(BF16).reshape(4, FAR, 512)
    for d in (1, 2, 3):
        for c in gather_two(d):
            c.start()
    listed[0, y] = chosen[0, y]
    listed[1, x] = chosen[1, x]

    act(PROLOGUE[3])
    for d in (1, 2, 3):
        for c in gather_two(d):
            c.wait_recv()
    act(PROLOGUE[4])

    lane_sel = lax.broadcasted_iota(jnp.int32, (FAR, 128), 1)
    far_row = lax.broadcasted_iota(jnp.int32, (FAR, 1), 0)
    lvl[...] = jnp.zeros_like(lvl)
    low_gap = jnp.where(me == 0, BIG, 0.0).astype(F32)
    high_gap = jnp.where(me == BLOCKS - 1, BIG, 0.0).astype(F32)
    gaps = (low_gap, None, None, high_gap, None)
    factor = SCALE * LOG2E

    def head(p, h):
        lanes = slice(h * DIM, h * DIM + DIM)
        head_no = 2 * p + h
        head_lanes = pl.ds(pl.multiple_of(head_no * DIM, DIM), DIM)
        bias = jnp.where(
            far_row < 16, bias_ref[0, head_no] + math.log(128),
            jnp.where(far_row < 24, bias_ref[1, head_no] + math.log(256),
                      jnp.where(far_row < 28, bias_ref[2, head_no] + math.log(512), -BIG)))
        bias = bias * LOG2E
        query = qx[p, :, lanes]
        grad = gx[p, :, lanes]
        top = None
        for (first, rows), gap in zip(CHUNKS, gaps):
            s = dot(kx[p, first : first + rows, lanes], query, NT) * factor
            if rows == FAR:
                s = s + bias
            s_ref[h, first : first + rows, :] = s
            peak = jnp.max(s, axis=0, keepdims=True)
            if gap is not None:
                peak = peak - gap
            top = peak if top is None else jnp.maximum(top, peak)
        total = jnp.zeros((1, LEAF), F32)
        for (first, rows), gap in zip(CHUNKS, gaps):
            base = top if gap is None else top + gap
            e = jnp.exp2(s_ref[h, first : first + rows, :] - base)
            s_ref[h, first : first + rows, :] = e
            total = total + jnp.sum(e, axis=0, keepdims=True)
        inverse = 1.0 / total
        for first, rows in CHUNKS:
            w_ref[h, first : first + rows, :] = (s_ref[h, first : first + rows, :] * inverse).astype(BF16)
        out = dot(vx[p, :, lanes], w_ref[h], TN).T.astype(BF16)
        o_ref[:, head_lanes] = out
        ones = jnp.ones((8, DIM), F32)
        row_dot = lax.dot_general(
            ones, out.astype(F32) * grad.astype(F32), NT,
            precision=lax.Precision.HIGHEST, preferred_element_type=F32)[0:1, :]
        for first, rows in CHUNKS:
            dw = dot(vx[p, first : first + rows, lanes], grad, NT)
            ds = s_ref[h, first : first + rows, :] * inverse * (dw - row_dot)
            d_ref[h, first : first + rows, :] = ds.astype(BF16)
            if rows == FAR:
                sums = jnp.sum(ds, axis=1, keepdims=True)
                lvl[...] += jnp.where(lane_sel == head_no, sums, 0.0)
        dq_ref[:, head_lanes] = (dot(kx[p, :, lanes], d_ref[h], TN) * SCALE).T.astype(BF16)
        dk = dot(d_ref[h], query) * SCALE
        dv = dot(w_ref[h], grad)
        for i, term in enumerate((dk, dv)):
            to_down[p, i, :, lanes] = term[:RIM].astype(BF16)
            own[p, i, :, lanes] = term[RIM : RIM + LEAF]
            to_up[p, i, :, lanes] = term[RIM + LEAF : NEAR].astype(BF16)
        return dk[NEAR:], dv[NEAR:]

    @pl.loop(0, PAIRS)
    def _(p):
        for i, dst in enumerate((kx, vx)):
            rows = listed[i, :, :, cols(p)].astype(F32)
            dst[p, NEAR:LIST, :] = ((rows[0] + rows[1]) + (rows[2] + rows[3])).astype(BF16)
        for c in load(p)[2:]:
            c.wait()
        for c in rims(p):
            c.wait_recv()

        def at_step(k, steps):
            if steps:
                @pl.when(p == k)
                def _():
                    act(steps)

        for k in range(PAIRS):
            at_step(k, BEFORE[k])
        first = head(p, 0)
        second = head(p, 1)
        for i, slot in ((0, y), (1, x)):
            dlisted[i, slot, :, cols(p)] = jnp.concatenate([first[i], second[i]], axis=1).astype(BF16)

        for k in range(PAIRS):
            at_step(k, AFTER[k])

    act(TAIL)

    swap.wait_recv()
    level_ref[...] = ((lvc[0] + lvc[1]) * (1.0 / math.sqrt(2 * BLOCKS * LEAF)))[0:3, 0:HEADS]

    swap.wait_send()
    for step in range(3):
        for c in level_steps(step):
            c.wait_send()
    for d in (1, 2, 3):
        gather_z(d).wait_send()
        for c in gather_one(d) + gather_two(d):
            c.wait_send()
        for part in (0, 1):
            for c in r1(part, d) + r2(part, d) + r3(part, d):
                c.wait_send()

    @pl.loop(0, PAIRS)
    def _(p):
        for c in rims(p) + back(p):
            c.wait_send()

    @pl.when((z == 0) | (z == 3))
    def _():
        for backward in (0, 1):
            for p in range(PAIRS):
                for i in (0, 1):
                    if (FWD_ROUTE, BWD_ROUTE)[backward][p][i]:
                        onward(p, i, backward)[0].wait_send()


def shards(queries, key_vectors, values, out_grad, far_lists, level_bias):
    any_spec = pl.BlockSpec(memory_space=pl.ANY)
    smem = pl.BlockSpec(memory_space=pltpu.SMEM)
    dma = pltpu.SemaphoreType.DMA
    outs = pl.pallas_call(
        kernel,
        out_shape=[pltpu.VMEM((LEAF, WIDTH), BF16)] * 4 + [pltpu.VMEM((3, HEADS), F32)],
        in_specs=[any_spec] * 4 + [smem] * 2,
        out_specs=[pl.BlockSpec(memory_space=pltpu.VMEM)] * 4 + [pl.BlockSpec(memory_space=pltpu.VMEM)],
        scratch_shapes=[
            pltpu.VMEM((PAIRS, LIST, PAIR), BF16),
            pltpu.VMEM((PAIRS, LIST, PAIR), BF16),
            pltpu.VMEM((PAIRS, LEAF, PAIR), BF16),
            pltpu.VMEM((PAIRS, LEAF, PAIR), BF16),
            pltpu.VMEM((PAIRS, 2, LEAF, PAIR), F32),
            pltpu.VMEM((PAIRS, 2, RIM, PAIR), BF16),
            pltpu.VMEM((PAIRS, 2, RIM, PAIR), BF16),
            pltpu.VMEM((PAIRS, 2, RIM, PAIR), BF16),
            pltpu.VMEM((PAIRS, 2, RIM, PAIR), BF16),
            pltpu.VMEM((2, 4, 16, WIDTH), BF16),
            pltpu.VMEM((2, 4, FAR, WIDTH), BF16),
            pltpu.VMEM((2, 4, FAR, WIDTH), BF16),
            pltpu.VMEM((2, 4, FAR, WIDTH), BF16),
            pltpu.VMEM((4, 8, WIDTH), F32),
            pltpu.VMEM((16, WIDTH), F32),
            pltpu.VMEM((2, 4, 16, WIDTH), BF16),
            pltpu.VMEM((2, 4, 16, WIDTH), BF16),
            pltpu.VMEM((4, 8, WIDTH), F32),
            pltpu.VMEM((4, 8, WIDTH), F32),
            pltpu.VMEM((8, WIDTH), F32),
            pltpu.VMEM((2, 4 * FAR, 64), BF16),
            pltpu.VMEM((FAR, 128), F32),
            pltpu.VMEM((4, 8, 128), F32),
            pltpu.VMEM((4, 8, 128), F32),
            pltpu.VMEM((4, 8, 128), F32),
            pltpu.VMEM((2, 8, 128), F32),
            pltpu.VMEM((2, LIST, LEAF), F32),
            pltpu.VMEM((2, LIST, LEAF), BF16),
            pltpu.VMEM((2, LIST, LEAF), BF16),
            pltpu.VMEM((PAIRS, 2, RIM, PAIR), BF16),
            pltpu.VMEM((PAIRS, 2, RIM, PAIR), BF16),
            dma((2, PAIRS, 2)), dma((2, PAIRS, 2)),
            dma((PAIRS, 2, 2)), dma((PAIRS, 2, 2)), dma((PAIRS, 2, 2)), dma((PAIRS, 2, 2)),
            dma((PAIRS, 4)),
            dma((3,)), dma((3,)), dma((2, 3)), dma((2, 3)), dma((2, 3)), dma((2, 3)),
            dma((2, 2, 3)), dma((2, 2, 3)), dma((2, 2, 3)), dma((2, 2, 3)), dma((2, 3)), dma((2, 3)),
            dma((3, 3)), dma((3, 3)), dma, dma,
        ],
        compiler_params=pltpu.CompilerParams(
            collective_id=0, has_side_effects=True, vmem_limit_bytes=54 * 1024 * 1024),
        cost_estimate=pl.CostEstimate(
            flops=12 * HEADS * LEAF * LIST * DIM, bytes_accessed=8 * LEAF * WIDTH * 2,
            transcendentals=HEADS * LEAF * LIST),
    )(queries[0], key_vectors[0], values[0], out_grad[0], far_lists.transpose(2, 0, 1), level_bias)
    return tuple(o[None] for o in outs[:4]) + (outs[4],)


def solution(mesh):
    token = P("batch", "seq", None)
    return jax.shard_map(
        shards,
        mesh=mesh,
        in_specs=(token, token, token, token, P("batch", None, None), P()),
        out_specs=(token, token, token, token, P()),
        check_vma=False,
    )
```
